512 devices in a mesh: sec: 2 (over core), frm: 32 (over y, x), clip: 8 (over z).
Axes of the slice: x: 4, y: 8, z: 8, core: 2. Of those that a mesh axis runs over, the one named last changes fastest.
Arguments:
- hidden: bfloat16 [8, 128, 64, 5120], P('clip', 'frm', None, 'sec'), may hold values from -150 to 150
- modulation: float32 [8, 2, 5120], P('clip', None, 'sec'), may hold values from -3 to 3
- head_w: bfloat16 [5120, 64], P('sec'), may hold values from -2 to 2
- clip_ids: int32 [8, 128], P('clip'), may hold values from 0 to 6, never falling along the last dimension, each value on 1 to 21 neighbouring positions
- w_in: bfloat16 [3, 16, 384], replicated, may hold values from -0.875 to 0.875
- gain_one: float32 [384], replicated, may hold values from 0.5 to 1.5
- w_one: bfloat16 [3, 384, 384], replicated, may hold values from -0.1875 to 0.1875
- w_up: bfloat16 [3, 384, 192], replicated, may hold values from -0.1875 to 0.1875
- gain_two: float32 [96], replicated, may hold values from 0.5 to 1.5
- w_two: bfloat16 [3, 96, 96], replicated, may hold values from -0.375 to 0.375
- reward_grad: bfloat16 [8, 256, 256, 96], P('clip', 'frm', 'sec'), may hold values from -6 to 6
Outputs:
- decoded: bfloat16 [8, 256, 256, 96], P('clip', 'frm', 'sec')
- hidden_grad: bfloat16 [8, 128, 64, 5120], P('clip', 'frm', None, 'sec')
The draws below stay inside these ranges and needn't reach their ends.
Inputs may be any that keep to these rules, and one draw needn't show every extreme that they name: `clip_ids`: ids never fall along a row; each clip spans 1 to min(21, 128) frames, and one spans exactly that many.
All inputs are finite; a program needn't handle non-finite values.
Results may differ from the reference program's by a relative error of at most 0.023.
Values may be sent and summed in bfloat16 or wider, within the bound.
A program may use at most 64 MiB of HBM per device.

```python
import math
import jax
import jax.numpy as jnp
import numpy as np
from jax import lax

DD = 5120
LAT = 16
C_HI = 384
C_LO = 96
PIXT = 64
FRAMES = 128
GROUPS = 8


def draw_hidden(key, part):
    key = jax.random.fold_in(key, 11)
    noise_key, row_key, col_key = jax.random.split(key, 3)
    shape = (GROUPS, FRAMES, PIXT, DD)
    row_scale = jnp.exp(jax.random.uniform(row_key, (GROUPS, FRAMES, PIXT, 1), jnp.float32, 0.0, math.log(10.0)))
    col_place = jnp.arange(DD, dtype=jnp.float32) / max(DD - 1, 1)
    group_place = jnp.arange(GROUPS, dtype=jnp.float32)[:, None, None, None] / max(GROUPS - 1, 1)
    frame_place = jnp.arange(FRAMES, dtype=jnp.float32)[None, :, None, None] / max(FRAMES - 1, 1)
    raw_noise = jax.random.normal(noise_key, shape, jnp.float32)
    falloff = 3.0
    rise = 5.0
    col_scale = jnp.power(rise, col_place) * jax.random.uniform(col_key, (DD,), jnp.float32, 0.75, 1.35)
    values = raw_noise * row_scale * col_scale * jnp.power(falloff, -(group_place + frame_place) / 2.0)
    return jnp.clip(values, -150.0, 150.0).astype(jnp.bfloat16)


def draw_head_w(key, part):
    key = jax.random.fold_in(key, 23)
    noise_key, common_key = jax.random.split(key, 2)
    shape = (DD, 4 * LAT)
    col_place = jnp.arange(DD, dtype=jnp.float32)[:, None] / max(DD - 1, 1)
    common = jnp.clip(jax.random.normal(common_key, (1, 4 * LAT), jnp.float32), -3.0, 3.0)
    noise = jnp.clip(jax.random.normal(noise_key, shape, jnp.float32), -4.0, 4.0)
    ramp = 0.5 + 2.0 * col_place
    values = (noise + common * ramp) / math.sqrt(DD)
    return jnp.clip(values, -2.0, 2.0).astype(jnp.bfloat16)


def shard_levels(stream_key, dims, shards, least, largest):
    def one(position, shards_of):
        heights = jax.random.uniform(jax.random.fold_in(jax.random.fold_in(stream_key, 6), position), (shards_of,), jnp.float32, least / len(shards), largest / len(shards))
        return jnp.repeat(jnp.exp(heights), dims[position] // shards_of).reshape((-1,) + (1,) * (len(dims) - position - 1))

    loudness = one(*shards[0])
    for cut in shards[1:]:
        loudness = loudness * one(*cut)
    return loudness


def split_up(count, total, most, slope):
    loads = [(1 << 20) // math.isqrt(rank ** slope) + 1 for rank in range(2, count + 1)]
    spare, given = total - most - (count - 1), [1] * (count - 1)
    while spare > 0:
        free = [i for i in range(count - 1) if given[i] < most]
        pool, left = sum([loads[i] for i in free]), spare
        for i in free:
            more = min(most - given[i], max(1, left * loads[i] // pool), spare)
            given[i] = given[i] + more
            spare = spare - more
    return np.array([most] + given)


def ragged(stream_key, number_of, total, most, lean):
    if number_of == 2:
        one = jax.random.randint(stream_key, (), max(1, total - most), min(most, total - 1) + 1)
        return jnp.stack([one, total - one])
    lengths = jnp.asarray(split_up(number_of, total, most, lean), jnp.int32)
    twos = (number_of - 1) // 2
    donor, taker = lengths[1:1 + 2 * twos:2], lengths[2:2 + 2 * twos:2]
    margin = jnp.minimum(donor - 1, most - taker)
    moved = jax.random.randint(jax.random.fold_in(stream_key, 1), (twos,), 0, 1 << 20) % (margin + 1)
    lengths = lengths.at[1:1 + 2 * twos:2].set(donor - moved).at[2:2 + 2 * twos:2].set(taker + moved)
    return lengths[jax.random.permutation(jax.random.fold_in(stream_key, 2), number_of)]


def gaussian(rng, extent, scale, limit, cuts=(), kind=jnp.bfloat16):
    array = jax.random.normal(rng, extent, jnp.float32) * scale
    if len(cuts) > 0:
        array = shard_levels(rng, extent, cuts, -0.22, 0.18) * array
    return jnp.clip(array, min=-limit, max=limit).astype(kind)


def setup_inputs(seed: int = 0) -> dict:
    arg_keys = jax.random.split(jax.random.key(seed), 12)
    return {
        "hidden": draw_hidden(jax.random.fold_in(arg_keys[11], 71), 0),
        "modulation": gaussian(arg_keys[1], (GROUPS, 2, DD), 0.5, 3.0, ((0, 8), (2, 2)), jnp.float32),
        "head_w": draw_head_w(jax.random.fold_in(arg_keys[11], 71), 0),
        "clip_ids": jax.vmap(lambda own: jnp.searchsorted(jnp.cumsum(ragged(own, (FRAMES + 20) // 21, FRAMES, min(21, FRAMES), 0)), jnp.arange(FRAMES), side="right"))(jax.random.split(arg_keys[3], GROUPS)).reshape((GROUPS, FRAMES)).astype(jnp.int32),
        "w_in": gaussian(arg_keys[4], (3, LAT, C_HI), (3 * LAT) ** -0.5, 0.875),
        "gain_one": jnp.clip(jax.random.uniform(arg_keys[5], (C_HI,), jnp.float32, 0.5, 1.5), 0.5, 1.5),
        "w_one": gaussian(arg_keys[6], (3, C_HI, C_HI), (3 * C_HI) ** -0.5, 0.1875),
        "w_up": gaussian(arg_keys[7], (3, C_HI, 2 * C_LO), (3 * C_HI) ** -0.5, 0.1875),
        "gain_two": jnp.clip(jax.random.uniform(arg_keys[8], (C_LO,), jnp.float32, 0.5, 1.5), 0.5, 1.5),
        "w_two": gaussian(arg_keys[9], (3, C_LO, C_LO), (3 * C_LO) ** -0.5, 0.375),
        "reward_grad": gaussian(arg_keys[10], (GROUPS, 2 * FRAMES, 4 * PIXT, C_LO), 1.0, 6.0, ((0, 8), (1, 32), (2, 2))),
    }


def seg_lookup(seg_row, frame_ids):
    total = seg_row.shape[0]
    hits = frame_ids[:, None] == jnp.arange(total, dtype=jnp.int32)[None, :]
    return lax.optimization_barrier(jnp.sum(jnp.where(hits, seg_row[None, :], 0), axis=1))

def frame_masks(seg_row, first, count):
    total = seg_row.shape[0]
    frame_ids = first + jnp.arange(count, dtype=jnp.int32)
    own_ids = seg_lookup(seg_row, frame_ids)
    inside = (frame_ids >= 0) & (frame_ids < total)
    stacked = []
    for offset in range(3):
        earlier = frame_ids - offset
        same = inside & (earlier >= 0) & (seg_lookup(seg_row, earlier) == own_ids)
        stacked.append(same.astype(jnp.float32))
    return jnp.stack(stacked)

def causal(extended, weight, mask_rows):
    length = extended.shape[0] - 2
    pixels = extended.shape[1]
    summed = jnp.zeros((length * pixels, weight.shape[2]), jnp.float32)
    for offset in range(3):
        shifted = extended[2 - offset:2 - offset + length] * mask_rows[offset][:, None, None].astype(extended.dtype)
        summed = summed + jnp.dot(shifted.reshape(length * pixels, -1), weight[offset], preferred_element_type=jnp.float32)
    return summed.reshape(length, pixels, -1)

def causal_back(extended, weight, mask_rows):
    length = extended.shape[0] - 2
    pixels = extended.shape[1]
    summed = jnp.zeros((length * pixels, weight.shape[1]), jnp.float32)
    for offset in range(3):
        picked = mask_rows[offset][offset:offset + length]
        shifted = extended[offset:offset + length] * picked[:, None, None].astype(extended.dtype)
        summed = summed + jnp.dot(shifted.reshape(length * pixels, -1), weight[offset].T, preferred_element_type=jnp.float32)
    return summed.reshape(length, pixels, -1)

def rms_silu(values, gain):
    inverse = lax.rsqrt(lax.optimization_barrier(jnp.mean(values * values, axis=-1, keepdims=True)) + 1e-06)
    normed = values * inverse * gain
    return (normed * jax.nn.sigmoid(normed)).astype(jnp.bfloat16)

def rms_silu_back(grads, values, gain):
    inverse = lax.rsqrt(lax.optimization_barrier(jnp.mean(values * values, axis=-1, keepdims=True)) + 1e-06)
    normed = values * inverse * gain
    sigmoid_part = jax.nn.sigmoid(normed)
    weighted = grads * sigmoid_part * (1.0 + normed * (1.0 - sigmoid_part)) * gain
    return inverse * weighted - values * inverse * inverse * inverse * lax.optimization_barrier(jnp.mean(weighted * values, axis=-1, keepdims=True))

def widen_kernel(w_in):
    identity = jnp.eye(4, dtype=w_in.dtype)
    return jnp.stack([jnp.kron(identity, w_in[offset]) for offset in range(3)])

def decode_forward(latent, first, seg_row, seg_two, weights, before):
    w_big, gain_one, w_one, w_up, gain_two, w_two = weights
    frames = latent.shape[0]
    tokens = latent.shape[1]
    lat_masks = frame_masks(seg_row, first, frames)
    out_masks = frame_masks(seg_two, 2 * first, 2 * frames)
    lat_ext = jnp.concatenate([before(latent, 0), latent])
    base = causal(lat_ext, w_big, lat_masks).reshape(frames, 4 * tokens, -1).astype(jnp.bfloat16)
    act_one = rms_silu(base.astype(jnp.float32), gain_one)
    trunk = base.astype(jnp.float32) + causal(jnp.concatenate([before(act_one, 1), act_one]), w_one, lat_masks)
    trunk = trunk.astype(jnp.bfloat16)
    raised = causal(jnp.concatenate([before(trunk, 2), trunk]), w_up, lat_masks)
    pixels = raised.shape[1]
    upsampled = raised.reshape(frames, pixels, 2, -1).transpose(0, 2, 1, 3).reshape(2 * frames, pixels, -1)
    upsampled = upsampled.astype(jnp.bfloat16)
    act_two = rms_silu(upsampled.astype(jnp.float32), gain_two)
    decoded = upsampled.astype(jnp.float32) + causal(jnp.concatenate([before(act_two, 3), act_two]), w_two, out_masks)
    return (base, upsampled, decoded.astype(jnp.bfloat16))

def decode_backward(reward_grad, base, upsampled, first, seg_row, seg_two, weights, after):
    w_big, gain_one, w_one, w_up, gain_two, w_two = weights
    frames = base.shape[0]
    tokens = base.shape[1] // 4
    lat_masks = frame_masks(seg_row, first, frames + 2)
    out_masks = frame_masks(seg_two, 2 * first, 2 * frames + 2)
    second_grad = causal_back(jnp.concatenate([reward_grad, after(reward_grad, 2, 0)]), w_two, out_masks)
    up_grad = reward_grad.astype(jnp.float32) + rms_silu_back(second_grad, upsampled.astype(jnp.float32), gain_two)
    up_grad = up_grad.astype(jnp.bfloat16)
    up_ext = jnp.concatenate([up_grad, after(up_grad, 4, 1)])
    pixels = up_ext.shape[1]
    folded = up_ext.reshape(frames + 2, 2, pixels, -1).transpose(0, 2, 1, 3).reshape(frames + 2, pixels, -1)
    trunk_grad = causal_back(folded, w_up, lat_masks).astype(jnp.bfloat16)
    first_grad = causal_back(jnp.concatenate([trunk_grad, after(trunk_grad, 2, 2)]), w_one, lat_masks)
    base_grad = trunk_grad.astype(jnp.float32) + rms_silu_back(first_grad, base.astype(jnp.float32), gain_one)
    base_grad = base_grad.astype(jnp.bfloat16)
    base_ext = jnp.concatenate([base_grad, after(base_grad, 2, 3)])
    latent_grad = causal_back(base_ext.reshape(frames + 2, tokens, -1), w_big, lat_masks)
    return latent_grad.astype(jnp.bfloat16)

def zero_prior(values, phase_number):
    return jnp.zeros_like(values[-2:])

def zero_later(values, count, phase_number):
    return jnp.zeros_like(values[:count])

def reference(hidden, modulation, head_w, clip_ids, w_in, gain_one, w_one, w_up, gain_two, w_two, reward_grad):
    weights = (widen_kernel(w_in), gain_one, w_one, w_up, gain_two, w_two)

    def one_group(items):
        group_hidden, group_mod, seg_row, group_reward = items
        seg_two = jnp.repeat(seg_row, 2)
        values = group_hidden.astype(jnp.float32)
        mean = lax.optimization_barrier(jnp.sum(values, axis=-1, keepdims=True)) / DD
        inverse = lax.rsqrt(lax.optimization_barrier(jnp.sum(values * values, axis=-1, keepdims=True)) / DD - mean * mean + 1e-06)
        normed = (values - mean) * inverse
        modulated = (normed * (1.0 + group_mod[1]) + group_mod[0]).astype(jnp.bfloat16)
        latent = jnp.dot(modulated.reshape(-1, DD), head_w, preferred_element_type=jnp.float32)
        latent = latent.reshape(FRAMES, PIXT, 4 * LAT).astype(jnp.bfloat16)
        base, upsampled, decoded = decode_forward(latent, 0, seg_row, seg_two, weights, zero_prior)
        latent_grad = decode_backward(group_reward, base, upsampled, 0, seg_row, seg_two, weights, zero_later)
        normed_grad = jnp.dot(latent_grad.reshape(-1, 4 * LAT), head_w.T, preferred_element_type=jnp.float32)
        normed_grad = normed_grad.reshape(FRAMES, PIXT, DD) * (1.0 + group_mod[1])
        first_sum = lax.optimization_barrier(jnp.sum(normed_grad, axis=-1, keepdims=True)) / DD
        second_sum = lax.optimization_barrier(jnp.sum(normed_grad * normed, axis=-1, keepdims=True)) / DD
        token_grad = inverse * (normed_grad - first_sum - normed * second_sum)
        return (decoded, token_grad)
    decoded, token_grad = lax.map(one_group, (hidden, modulation, clip_ids, reward_grad))
    count = float(GROUPS * FRAMES * PIXT * DD)
    total = jnp.sum(token_grad * token_grad)
    hidden_grad = (token_grad * lax.rsqrt(total / count + 1e-06)).astype(jnp.bfloat16)
    return (decoded, hidden_grad)
```

```python
import functools

import jax
import jax.numpy as jnp
from jax import lax
from jax.experimental import pallas as pl
from jax.experimental.pallas import tpu as pltpu
from jax.sharding import PartitionSpec as P

BF = jnp.bfloat16
F32 = jnp.float32
MESH = pl.DeviceIdType.MESH
HI = 384
LO = 96
EPS = 1e-6
RB = 64


def nn(a, b):
    return jnp.dot(a, b, preferred_element_type=F32)


def nt(a, b):
    return lax.dot_general(a, b, (((1,), (1,)), ((), ())), preferred_element_type=F32)


def iota(shape, dim):
    return lax.broadcasted_iota(jnp.int32, shape, dim)


def one_hot(cond):
    return jnp.where(cond, 1.0, 0.0).astype(BF)


def sigmoid(x):
    return 0.5 * jnp.tanh(0.5 * x) + 0.5


def tile(mask, times):
    return jnp.concatenate([mask] * times, axis=1)


def nb(x, gain, width):
    r = lax.rsqrt(jnp.sum(x * x, axis=-1, keepdims=True) * (1.0 / width) + EPS)
    n = x * r * gain
    return n * sigmoid(n)


def nb_back(g, x, gain, width):
    r = lax.rsqrt(jnp.sum(x * x, axis=-1, keepdims=True) * (1.0 / width) + EPS)
    n = x * r * gain
    sg = sigmoid(n)
    u = g * sg * (1.0 + n * (1.0 - sg)) * gain
    mixed = jnp.sum(u * x, axis=-1, keepdims=True) * (1.0 / width)
    return r * u - x * (r * r * r * mixed)


def main_kernel(
    nf, nc, dd, count,
    hidden, mod, head_w, ids, w_in, gain1, w_one, w_up, gain2, w_two, reward,
    coef, wr, rd,
    HX, HW, W1, WUR, RWI, XS, XR, X2, RX, SRC, SR, RW, LTS, MT, MS, REP, WD, WI, WUP, G2,
    B, AC, TR, U, UP, A2, DEC, HS, UG, JL, TG, BG, ZM, PS, X3, RXA, ZS, ZB, ST,
    lsem, sec_s, sec_r, lat_s, lat_r, rew_s, rew_r, dec_s, dec_r, lg_s, lg_r, sx_s, sx_r, z_s, z_r,
):
    sec = lax.axis_index("sec")
    frm = lax.axis_index("frm")
    clip = lax.axis_index("clip")
    rows = 16 * nf
    line = 4 * nf
    hr = 8 * nf
    steps = rows // RB

    loads = [
        pltpu.make_async_copy(head_w, HW, lsem.at[0]),
        pltpu.make_async_copy(hidden, HX.at[pl.ds(0, hr)], lsem.at[1]),
        pltpu.make_async_copy(reward, RWI, lsem.at[2]),
        pltpu.make_async_copy(w_up, WUR, lsem.at[3]),
        pltpu.make_async_copy(w_one, W1, lsem.at[4]),
    ]
    for load in loads:
        load.start()

    barrier = pltpu.get_barrier_semaphore()

    def greet_frm(q, c):
        pl.semaphore_signal(barrier, inc=1, device_id=(sec, lax.rem(frm + q, nf), clip), device_id_type=MESH)
        return c

    lax.fori_loop(1, nf, greet_frm, 0)

    def cross(q):
        other = lax.rem(sec * nc + clip + q, 2 * nc)
        return (other // nc, frm, lax.rem(other, nc))

    def greet_cross(q, c):
        pl.semaphore_signal(barrier, inc=1, device_id=cross(q), device_id_type=MESH)
        return c

    lax.fori_loop(1, 2 * nc, greet_cross, 0)

    def to_all(src, dst, ssem, rsem):
        def send(q, c):
            d = lax.rem(frm + q, nf)
            pltpu.make_async_remote_copy(
                src_ref=src.at[d], dst_ref=dst.at[frm], send_sem=ssem, recv_sem=rsem,
                device_id=(sec, d, clip), device_id_type=MESH,
            ).start()
            return c

        lax.fori_loop(1, nf, send, 0)

    def all_of(src, dst, ssem, rsem):
        return pltpu.make_async_remote_copy(
            src_ref=src.at[pl.ds(0, nf - 1)], dst_ref=dst.at[pl.ds(0, nf - 1)],
            send_sem=ssem, recv_sem=rsem, device_id=(sec, frm, clip), device_id_type=MESH,
        )

    HX[pl.ds(hr + 64, 16), :] = jnp.ones((16, HX.shape[1]), BF)
    HX[pl.ds(hr + 80, 48), :] = jnp.zeros((48, HX.shape[1]), BF)
    loads[0].wait()
    shift = mod[0:1, :]
    scaled = nt(one_hot(iota((64, 64), 0) == iota((64, 64), 1)), HW[...]) * (1.0 + mod[1:2, :])
    scaled = scaled.astype(BF)
    HX[pl.ds(hr, 64), :] = scaled
    wr[...] = scaled
    coarse = shift.astype(BF).astype(F32)
    pick = iota((16, HX.shape[1]), 0)
    pair = jnp.where(pick == 0, coarse, jnp.where(pick == 1, shift - coarse, 0.0)).astype(BF)
    shifted = nn(pair, HW[...])
    loads[1].wait()
    product = nt(HX[pl.ds(0, hr + 80), :], HX[pl.ds(hr, 128), :])
    XS[pl.ds(0, hr + 80), :] = product
    XS[pl.ds(hr + 72, 8), pl.ds(0, 64)] = jnp.broadcast_to(shifted[0:1, :] + shifted[1:2, :], (8, 64))

    def squares(b, c):
        at = pl.multiple_of(b * 16, 16)
        x = HX[pl.ds(at, 16), :].astype(F32)
        total = jnp.sum(x * x, axis=-1, keepdims=True)
        XS[pl.ds(at, 16), :] += jnp.where(iota((16, 128), 1) == 80, total, 0.0)
        return c

    lax.fori_loop(0, hr // 16, squares, 0)

    pl.semaphore_wait(barrier, nf - 1 + 2 * nc - 1)
    swap = pltpu.make_async_remote_copy(
        src_ref=XS, dst_ref=XR, send_sem=sec_s, recv_sem=sec_r,
        device_id=(1 - sec, frm, clip), device_id_type=MESH,
    )
    swap.start()

    when = iota((line, 128), 0)
    own = jnp.broadcast_to(ids[...].astype(F32), (128, line)).T
    mt1 = jnp.where((own == pltpu.roll(own, 1, 0)) & (when >= 1), 1.0, 0.0)
    mt2 = jnp.where((own == pltpu.roll(own, 2, 0)) & (when >= 2), 1.0, 0.0)
    mt1u = pltpu.roll(mt1, line - 1, 0)
    mt2u = pltpu.roll(mt2, line - 2, 0)
    masks = jnp.concatenate([mt1, mt2, mt1u, mt2u], axis=1)
    MT[...] = masks
    REP[...] = one_hot(iota((rows, line), 0) // 4 == iota((rows, line), 1))
    MS[...] = nn(REP[...], masks.astype(BF))

    WD[...] = jnp.zeros(WD.shape, BF)
    WD[pl.ds(0, LO), pl.ds(0, LO)] = w_two[0]
    WD[pl.ds(0, LO), pl.ds(128, LO)] = w_two[1]
    WD[pl.ds(128, LO), pl.ds(128, LO)] = w_two[0]
    WD[pl.ds(256, LO), pl.ds(0, LO)] = w_two[2]
    WD[pl.ds(384, LO), pl.ds(0, LO)] = w_two[1]
    WD[pl.ds(384, LO), pl.ds(128, LO)] = w_two[2]
    WI[...] = jnp.zeros(WI.shape, BF)
    for k in range(3):
        for s in range(4):
            WI[pl.ds(128 * k + 16 * s, 16), :] = w_in[k]
    G2[...] = jnp.zeros(G2.shape, F32)
    G2[:, pl.ds(0, LO)] = jnp.broadcast_to(gain2[...], (8, LO))
    U[:, pl.ds(0, 8), :] = jnp.zeros((3, 8, 256), F32)
    HS[pl.ds(rows, 8), :] = jnp.zeros((8, 512), F32)
    JL[pl.ds(rows, 8), :] = jnp.zeros((8, 3 * HI), F32)

    loads[2].wait()
    SRC[...] = jnp.zeros(SRC.shape, BF)
    for j in range(4):
        for i in range(2):
            SRC[pl.ds(j * 4 * nf, 4 * nf), pl.ds(128 * i, LO)] = RWI[2 * j + i]
    to_row = iota((rows, rows), 0)
    from_row = iota((rows, rows), 1)
    perm = one_hot(from_row == ((to_row & 15) // 4) * (4 * nf) + (to_row // 16) * 4 + (to_row & 3))
    SR[...] = nn(perm, SRC[...]).astype(BF).reshape(nf, 16, 256)
    loads[3].wait()
    lane = iota((2 * LO, 256), 1)
    place = one_hot(((lane & 127) < LO) & (iota((2 * LO, 256), 0) == (lane // 128) * LO + (lane & 127)))
    WUP[...] = nn(WUR[...], place).astype(BF)

    swap.wait()
    ST[...] = XS[...] + XR[...]
    consts = ST[pl.ds(hr + 64, 16), :]
    col_sum = consts[0:1, :]
    sw = consts[8:9, :]
    stats = ST[pl.ds(0, hr), :]
    mean = stats[:, 64:65] * (1.0 / dd)
    inv = lax.rsqrt(stats[:, 80:81] * (1.0 / dd) - mean * mean + EPS)
    hl = iota((hr, 128), 1)
    pay = jnp.where(hl < 64, inv * (stats - mean * col_sum), jnp.where(hl == 64, inv, 0.0))
    XS[pl.ds(0, hr), :] = pay
    for j in range(4):
        X2[:, j, :] = XS[pl.ds(pl.multiple_of(j * 2 * nf + sec * nf, 8) if nf % 8 == 0 else j * 2 * nf + sec * nf, nf), :]
    to_all(X2, RX, lat_s, lat_r)
    to_all(SR, RW, rew_s, rew_r)
    RX[pl.ds(frm, 1)] = X2[pl.ds(frm, 1)]
    RW[pl.ds(frm, 1)] = SR[pl.ds(frm, 1)]
    all_of(X2, RX, lat_s, lat_r).wait_recv()

    for j in range(4):
        LTS[pl.ds(j, nf, stride=4), :] = RX[:, j, :]
    tl = iota((line, 128), 1)
    lat = jnp.where(tl < 64, LTS[...] + sw, 0.0)
    lat = lat.astype(BF).astype(F32)
    cat = jnp.concatenate(
        [lat, MT[:, 0:128] * pltpu.roll(lat, 1, 0), MT[:, 128:256] * pltpu.roll(lat, 2, 0)], axis=1
    ).astype(BF)
    mine = ((iota((rows, HI), 1) & 127) // 16) == (iota((rows, HI), 0) & 3)
    spread = jnp.where(mine, nn(REP[...], cat), 0.0).astype(BF)
    B[...] = nn(spread, WI[...])
    g1 = gain1[...]

    def act_one(b, carry):
        at = pl.multiple_of(b * RB, RB)
        act = nb(B[pl.ds(at, RB), :], g1, HI)
        ext = jnp.concatenate([carry, act], axis=0)
        m1 = tile(MS[pl.ds(at, RB), 0:128], 3)
        m2 = tile(MS[pl.ds(at, RB), 128:256], 3)
        AC[pl.ds(at, RB), 0:HI] = act.astype(BF)
        AC[pl.ds(at, RB), HI : 2 * HI] = (ext[4 : RB + 4] * m1).astype(BF)
        AC[pl.ds(at, RB), 2 * HI : 3 * HI] = (ext[0:RB] * m2).astype(BF)
        return ext[RB:]

    lax.fori_loop(0, steps, act_one, jnp.zeros((8, HI), F32))
    loads[4].wait()
    TR[...] = (B[...] + nn(AC[...], W1[...])).astype(BF)
    for k in range(3):
        U[k, pl.ds(8, rows), :] = nn(TR[...], WUP[pl.ds(HI * k, HI), :])
    g2 = G2[0:1, :]

    def act_two(b, carry):
        at = pl.multiple_of(b * RB, RB)
        m1 = tile(MS[pl.ds(at, RB), 0:128], 2)
        m2 = tile(MS[pl.ds(at, RB), 128:256], 2)
        one = U[1, pl.ds(at, RB + 8), :]
        two = U[2, pl.ds(at, RB + 8), :]
        up = U[0, pl.ds(at + 8, RB), :] + one[4 : RB + 4] * m1 + two[0:RB] * m2
        UP[pl.ds(at, RB), :] = up
        act = jnp.concatenate([nb(up[:, :128], g2, LO), nb(up[:, 128:], g2, LO)], axis=1)
        ext = jnp.concatenate([carry, act], axis=0)
        A2[pl.ds(at, RB), 0:256] = act.astype(BF)
        A2[pl.ds(at, RB), 256:512] = (ext[4 : RB + 4] * m1).astype(BF)
        return ext[RB:]

    lax.fori_loop(0, steps, act_two, jnp.zeros((8, 256), F32))
    DEC[...] = (UP[...] + nn(A2[...], WD[...])).astype(BF).reshape(nf, 16, 256)
    to_all(DEC, rd, dec_s, dec_r)
    keep = pltpu.make_async_copy(DEC.at[frm], rd.at[frm], lsem.at[5])
    keep.start()

    all_of(SR, RW, rew_s, rew_r).wait_recv()
    HS[pl.ds(0, rows), :] = nt(RW[...].reshape(rows, 256), WD[...])

    def up_grad(b, c):
        at = pl.multiple_of(b * RB, RB)
        m1 = tile(MS[pl.ds(at, RB), 256:384], 2)
        later = HS[pl.ds(at, RB + 8), 256:512]
        second = HS[pl.ds(at, RB), 0:256] + later[4 : RB + 4] * m1
        up = UP[pl.ds(at, RB), :]
        g = RW[pl.ds(b * (RB // 16), RB // 16)].reshape(RB, 256).astype(F32)
        back = [nb_back(second[:, i : i + 128], up[:, i : i + 128], g2, LO) for i in (0, 128)]
        UG[pl.ds(at, RB), :] = (g + jnp.concatenate(back, axis=1)).astype(BF)
        return c

    lax.fori_loop(0, steps, up_grad, 0)
    JL[pl.ds(0, rows), :] = nt(UG[...], WUP[...])

    def gathered(at):
        m1 = tile(MS[pl.ds(at, RB), 256:384], 3)
        m2 = tile(MS[pl.ds(at, RB), 384:512], 3)
        one = JL[pl.ds(at, RB + 8), HI : 2 * HI]
        two = JL[pl.ds(at, RB + 8), 2 * HI : 3 * HI]
        return JL[pl.ds(at, RB), 0:HI] + one[4 : RB + 4] * m1 + two[8 : RB + 8] * m2

    def trunk_grad(b, c):
        at = pl.multiple_of(b * RB, RB)
        TG[pl.ds(at, RB), :] = gathered(at).astype(BF)
        return c

    lax.fori_loop(0, steps, trunk_grad, 0)
    JL[pl.ds(0, rows), :] = nt(TG[...], W1[...])

    def base_grad(b, c):
        at = pl.multiple_of(b * RB, RB)
        back = nb_back(gathered(at), B[pl.ds(at, RB), :], g1, HI)
        BG[pl.ds(at, RB), :] = (TG[pl.ds(at, RB), :].astype(F32) + back).astype(BF)
        return c

    lax.fori_loop(0, steps, base_grad, 0)
    ZM[...] = jnp.where(mine, nt(BG[...], WI[...]), 0.0).astype(BF)
    rep_t = one_hot(iota((line, rows), 0) == iota((line, rows), 1) // 4)
    y = nn(rep_t, ZM[...])
    lg = y[:, 0:128]
    lg = lg + MT[:, 256:384] * pltpu.roll(y[:, 128:256], line - 1, 0)
    lg = lg + MT[:, 384:512] * pltpu.roll(y[:, 256:384], line - 2, 0)
    lgb = lg.astype(BF)
    lg = lgb.astype(F32)

    pre = LTS[...]
    inv_t = pre[:, 64:65]
    first = jnp.sum(lg * col_sum, axis=-1, keepdims=True) * (1.0 / dd)
    second = jnp.sum(lg * pre, axis=-1, keepdims=True) * (1.0 / dd)
    gram = ST[pl.ds(hr, 64), :]
    gram_hi = gram.astype(BF)
    gram_lo = (gram - gram_hi.astype(F32)).astype(BF)
    quad = nn(lgb[:, 0:64], gram_hi) + nn(lgb[:, 0:64], gram_lo)
    quad = jnp.sum(lg * quad, axis=-1, keepdims=True)
    inv_sq = inv_t * inv_t
    part = inv_sq * (quad - dd * (first * first + second * second * (1.0 + EPS * inv_sq)))
    part = jnp.sum(part, axis=0, keepdims=True)
    PS[...] = jnp.where(
        tl < 64, lg, jnp.where(tl == 64, first, jnp.where(tl == 65, second, jnp.where(tl == 66, part, 0.0)))
    )
    for j in range(4):
        X3[:, j, :] = PS[pl.ds(j, nf, stride=4), :]
    half = RXA.at[sec]
    to_all(X3, half, lg_s, lg_r)
    half[pl.ds(frm, 1)] = X3[pl.ds(frm, 1)]
    all_of(X3, half, lg_s, lg_r).wait_recv()

    trade = pltpu.make_async_remote_copy(
        src_ref=RXA.at[sec], dst_ref=RXA.at[sec], send_sem=sx_s, recv_sem=sx_r,
        device_id=(1 - sec, frm, clip), device_id_type=MESH,
    )
    trade.start()
    ZS[...] = jnp.broadcast_to(jnp.sum(half[:, 0, :], axis=0, keepdims=True), (8, 128))
    slot = sec * nc + clip

    def send_total(q, c):
        pltpu.make_async_remote_copy(
            src_ref=ZS, dst_ref=ZB.at[slot], send_sem=z_s, recv_sem=z_r,
            device_id=cross(q), device_id_type=MESH,
        ).start()
        return c

    lax.fori_loop(1, 2 * nc, send_total, 0)
    ZB[pl.ds(slot, 1)] = ZS[...].reshape(1, 8, 128)
    trade.wait()
    for j in range(4):
        for s in range(2):
            coef[pl.ds(j * 2 * nf + s * nf, nf), :] = RXA[s, :, j, :]
    z_all = pltpu.make_async_remote_copy(
        src_ref=ZB.at[pl.ds(0, 2 * nc - 1)], dst_ref=ZB.at[pl.ds(0, 2 * nc - 1)],
        send_sem=z_s, recv_sem=z_r, device_id=(sec, frm, clip), device_id_type=MESH,
    )
    z_all.wait_recv()
    total = jnp.sum(ZB[...], axis=0)[0:1, 66:67]
    grow = lax.rsqrt(jnp.maximum(total, 0.0) * (1.0 / count) + EPS)
    got = coef[...]
    a = got[:, 64:65]
    b = got[:, 65:66]
    stats = ST[pl.ds(0, hr), :]
    mean = stats[:, 64:65] * (1.0 / dd)
    inv = lax.rsqrt(stats[:, 80:81] * (1.0 / dd) - mean * mean + EPS)
    k0 = inv * grow
    k1 = k0 * (inv * b * mean - a)
    k2 = k0 * inv * b
    coef[...] = jnp.where(
        hl < 64, got, jnp.where(hl == 64, k0, jnp.where(hl == 65, k1, jnp.where(hl == 66, k2, 0.0)))
    )

    keep.wait()
    all_of(DEC, rd, dec_s, dec_r).wait_recv()
    all_of(X2, RX, lat_s, lat_r).wait_send()
    all_of(SR, RW, rew_s, rew_r).wait_send()
    all_of(DEC, rd, dec_s, dec_r).wait_send()
    all_of(X3, half, lg_s, lg_r).wait_send()
    z_all.wait_send()


def last_kernel(nf, coef, wr, hidden, rd, out, decoded):
    got = coef[...]
    grads = nn(got[:, 0:64].astype(BF), wr[...])
    out[...] = (grads * got[:, 64:65] + got[:, 65:66] - hidden[...].astype(F32) * got[:, 66:67]).astype(BF)

    @pl.when(pl.program_id(0) == 0)
    def _():
        rows = 16 * nf
        to_row = iota((rows, rows), 0)
        from_row = iota((rows, rows), 1)
        edge = 4 * nf
        perm = one_hot(from_row == ((lax.rem(to_row, edge)) // 4) * 16 + (to_row // edge) * 4 + (to_row & 3))
        back = nn(perm, rd[...].reshape(rows, 256)).astype(BF)
        for j in range(4):
            for i in range(2):
                decoded[2 * j + i] = back[j * edge : (j + 1) * edge, 128 * i : 128 * i + LO]


def body(nf, nc, dd, count, hidden, modulation, head_w, clip_ids, w_in, gain_one, w_one, w_up, gain_two, w_two, reward_grad):
    wide = hidden.shape[3]
    rows, line, hr = 16 * nf, 4 * nf, 8 * nf
    hid = hidden.reshape(hr, wide)
    anyspace = pl.BlockSpec(memory_space=pl.ANY)
    vm = pl.BlockSpec(memory_space=pltpu.VMEM)
    dma = pltpu.SemaphoreType.DMA
    V = pltpu.VMEM
    coef, wr, rd = pl.pallas_call(
        functools.partial(main_kernel, nf, nc, dd, count),
        out_shape=(
            jax.ShapeDtypeStruct((hr, 128), F32),
            jax.ShapeDtypeStruct((64, wide), BF),
            jax.ShapeDtypeStruct((nf, 16, 256), BF),
        ),
        in_specs=[anyspace, vm, anyspace, vm, vm, vm, anyspace, anyspace, vm, vm, anyspace],
        out_specs=(vm, vm, anyspace),
        scratch_shapes=[
            V((hr + 128, wide), BF),
            V((wide, 64), BF),
            V((3 * HI, HI), BF),
            V((3 * HI, 2 * LO), BF),
            V((8, 4 * nf, LO), BF),
            V((hr + 80, 128), F32),
            V((hr + 80, 128), F32),
            V((nf, 4, 128), F32),
            V((nf, 4, 128), F32),
            V((rows, 256), BF),
            V((nf, 16, 256), BF),
            V((nf, 16, 256), BF),
            V((line, 128), F32),
            V((line, 512), F32),
            V((rows, 512), F32),
            V((rows, line), BF),
            V((512, 256), BF),
            V((HI, HI), BF),
            V((3 * HI, 256), BF),
            V((8, 128), F32),
            V((rows, HI), F32),
            V((rows, 3 * HI), BF),
            V((rows, HI), BF),
            V((3, rows + 8, 256), F32),
            V((rows, 256), F32),
            V((rows, 512), BF),
            V((nf, 16, 256), BF),
            V((rows + 8, 512), F32),
            V((rows, 256), BF),
            V((rows + 8, 3 * HI), F32),
            V((rows, HI), BF),
            V((rows, HI), BF),
            V((rows, HI), BF),
            V((line, 128), F32),
            V((nf, 4, 128), F32),
            V((2, nf, 4, 128), F32),
            V((8, 128), F32),
            V((2 * nc, 8, 128), F32),
            V((hr + 80, 128), F32),
            dma((6,)),
        ]
        + [dma] * 14,
        compiler_params=pltpu.CompilerParams(
            collective_id=0, has_side_effects=True, vmem_limit_bytes=48 * 1024 * 1024
        ),
        name="exchange",
    )(
        hid, modulation[0], head_w, clip_ids, w_in, gain_one[None], w_one.reshape(3 * HI, HI),
        w_up.reshape(3 * HI, 2 * LO), gain_two[None], w_two, reward_grad[0],
    )
    cut = 512 if wide % 512 == 0 else wide
    grad, decoded = pl.pallas_call(
        functools.partial(last_kernel, nf),
        grid=(wide // cut,),
        out_shape=(
            jax.ShapeDtypeStruct((hr, wide), BF),
            jax.ShapeDtypeStruct((8, 4 * nf, LO), BF),
        ),
        in_specs=[
            pl.BlockSpec((hr, 128), lambda i: (0, 0)),
            pl.BlockSpec((64, cut), lambda i: (0, i)),
            pl.BlockSpec((hr, cut), lambda i: (0, i)),
            pl.BlockSpec((nf, 16, 256), lambda i: (0, 0, 0)),
        ],
        out_specs=(
            pl.BlockSpec((hr, cut), lambda i: (0, i)),
            pl.BlockSpec((8, 4 * nf, LO), lambda i: (0, 0, 0)),
        ),
        compiler_params=pltpu.CompilerParams(vmem_limit_bytes=32 * 1024 * 1024),
        name="finish",
    )(coef, wr, hid, rd)
    return decoded[None], grad.reshape(hidden.shape)


def solution(mesh):
    nf, nc = mesh.shape["frm"], mesh.shape["clip"]

    def whole(hidden, *rest):
        dd = hidden.shape[3]
        count = float(hidden.size)
        in_specs = (
            P("clip", "frm", None, "sec"),
            P("clip", None, "sec"),
            P("sec", None),
            P("clip", None),
            P(),
            P(),
            P(),
            P(),
            P(),
            P(),
            P("clip", "frm", "sec", None),
        )
        out_specs = (P("clip", "frm", "sec", None), P("clip", "frm", None, "sec"))
        return jax.shard_map(
            functools.partial(body, nf, nc, dd, count),
            mesh=mesh, in_specs=in_specs, out_specs=out_specs, check_vma=False,
        )(hidden, *rest)

    return whole
```

```python
import functools

import jax
import jax.numpy as jnp
from jax import lax
from jax.experimental import pallas as pl
from jax.experimental.pallas import tpu as pltpu
from jax.sharding import PartitionSpec as P

BF = jnp.bfloat16
F32 = jnp.float32
MESH = pl.DeviceIdType.MESH
HI = 384
LO = 96
EPS = 1e-6
RB = 64


def nn(a, b):
    return jnp.dot(a, b, preferred_element_type=F32)


def nt(a, b):
    return lax.dot_general(a, b, (((1,), (1,)), ((), ())), preferred_element_type=F32)


def iota(shape, dim):
    return lax.broadcasted_iota(jnp.int32, shape, dim)


def one_hot(cond):
    return jnp.where(cond, 1.0, 0.0).astype(BF)


def sigmoid(x):
    return 0.5 * jnp.tanh(0.5 * x) + 0.5


def tile(mask, times):
    return jnp.concatenate([mask] * times, axis=1)


def nb(x, gain, width):
    r = lax.rsqrt(jnp.sum(x * x, axis=-1, keepdims=True) * (1.0 / width) + EPS)
    n = x * r * gain
    return n * sigmoid(n)


def nb_back(g, x, gain, width):
    r = lax.rsqrt(jnp.sum(x * x, axis=-1, keepdims=True) * (1.0 / width) + EPS)
    n = x * r * gain
    sg = sigmoid(n)
    u = g * sg * (1.0 + n * (1.0 - sg)) * gain
    mixed = jnp.sum(u * x, axis=-1, keepdims=True) * (1.0 / width)
    return r * u - x * (r * r * r * mixed)


def main_kernel(
    nf, nc, dd, count,
    hidden, mod, head_w, ids, w_in, gain1, w_one, w_up, gain2, w_two, reward,
    raw, scale_out, dect,
    HX, HW, W1, XS, XR, X2, RX, SRC, SR, RW, LTS, MT, MS, REP, WD, WI, WUP, G2,
    B, AC, TR, U, UP, A2, DEC, HS, UG, JL, TG, BG, ZM, PS, X3, RXA, ZS, ZB, ST, RD, FIN, KB, RAW, DT,
    lsem, sec_s, sec_r, lat_s, lat_r, rew_s, rew_r, dec_s, dec_r, lg_s, lg_r, sx_s, sx_r, z_s, z_r,
):
    sec = lax.axis_index("sec")
    frm = lax.axis_index("frm")
    clip = lax.axis_index("clip")
    rows = 16 * nf
    line = 4 * nf
    hr = 8 * nf
    steps = rows // RB

    edge = 4 * nf
    loads = [
        [pltpu.make_async_copy(head_w, HW, lsem.at[0])],
        [pltpu.make_async_copy(hidden, HX.at[pl.ds(0, hr)], lsem.at[1])],
        [
            pltpu.make_async_copy(
                reward.at[2 * j + i], SRC.at[pl.ds(128 * i, LO), pl.ds(j * edge, edge)], lsem.at[6 + 2 * j + i]
            )
            for j in range(4) for i in range(2)
        ],
        [
            pltpu.make_async_copy(
                w_up.at[k, pl.ds(LO * i, LO)], WUP.at[pl.ds(256 * k + 128 * i, LO)], lsem.at[14 + 2 * k + i]
            )
            for k in range(3) for i in range(2)
        ],
        [pltpu.make_async_copy(w_one, W1, lsem.at[4])],
    ]

    def load(which):
        for copy in loads[which]:
            copy.wait()

    for group in loads:
        for copy in group:
            copy.start()

    nx = 4
    ny = nf // nx
    yy, xx = frm // nx, lax.rem(frm, nx)
    far = sorted(
        ((min(dy, ny - dy) + min(dx, nx - dx), dy, dx) for dy in range(ny) for dx in range(nx) if dy or dx),
        reverse=True,
    )
    peers = [lax.rem(yy + dy, ny) * nx + lax.rem(xx + dx, nx) for _, dy, dx in far]
    above = [lax.rem(clip + dz, nc) for dz in sorted(range(1, nc), key=lambda dz: -min(dz, nc - dz))]

    barrier = pltpu.get_barrier_semaphore()
    for d in peers:
        pl.semaphore_signal(barrier, inc=1, device_id=(sec, d, clip), device_id_type=MESH)
    for d in above:
        pl.semaphore_signal(barrier, inc=1, device_id=(sec, frm, d), device_id_type=MESH)
    pl.semaphore_signal(barrier, inc=1, device_id=(1 - sec, frm, clip), device_id_type=MESH)

    def to_all(src, dst, ssem, rsem):
        for d in peers:
            pltpu.make_async_remote_copy(
                src_ref=src.at[d], dst_ref=dst.at[frm], send_sem=ssem, recv_sem=rsem,
                device_id=(sec, d, clip), device_id_type=MESH,
            ).start()

    def all_of(src, dst, ssem, rsem):
        return pltpu.make_async_remote_copy(
            src_ref=src.at[pl.ds(0, nf - 1)], dst_ref=dst.at[pl.ds(0, nf - 1)],
            send_sem=ssem, recv_sem=rsem, device_id=(sec, frm, clip), device_id_type=MESH,
        )

    HX[pl.ds(hr + 64, 16), :] = jnp.ones((16, HX.shape[1]), BF)
    HX[pl.ds(hr + 80, 48), :] = jnp.zeros((48, HX.shape[1]), BF)
    load(0)
    shift = mod[0:1, :]
    HX[pl.ds(hr, 64), :] = (HW[...].astype(F32) * (1.0 + mod[1:2, :])).astype(BF)
    coarse = shift.astype(BF).astype(F32)
    pick = iota((16, HX.shape[1]), 0)
    pair = jnp.where(pick == 0, coarse, jnp.where(pick == 1, shift - coarse, 0.0)).astype(BF)
    shifted = nt(pair, HW[...])
    XS[pl.ds(hr, 80), :] = nt(HX[pl.ds(hr, 80), :], HX[pl.ds(hr, 128), :])
    XS[pl.ds(hr + 72, 8), pl.ds(0, 64)] = jnp.broadcast_to(shifted[0:1, :] + shifted[1:2, :], (8, 64))

    load(1)
    block = min(hr, 64)
    for b in range(hr // block):
        h = HX[pl.ds(b * block, block), :]
        x = h.astype(F32)
        total = jnp.sum(x * x, axis=-1, keepdims=True)
        XS[pl.ds(b * block, block), :] = nt(h, HX[pl.ds(hr, 128), :]) + jnp.where(
            iota((block, 128), 1) == 80, total, 0.0
        )

    pl.semaphore_wait(barrier, nf - 1 + nc)
    swap = pltpu.make_async_remote_copy(
        src_ref=XS, dst_ref=XR, send_sem=sec_s, recv_sem=sec_r,
        device_id=(1 - sec, frm, clip), device_id_type=MESH,
    )
    swap.start()

    when = iota((line, 128), 0)
    own = jnp.broadcast_to(ids[...].astype(F32), (128, line)).T
    mt1 = jnp.where((own == pltpu.roll(own, 1, 0)) & (when >= 1), 1.0, 0.0)
    mt2 = jnp.where((own == pltpu.roll(own, 2, 0)) & (when >= 2), 1.0, 0.0)
    mt1u = pltpu.roll(mt1, line - 1, 0)
    mt2u = pltpu.roll(mt2, line - 2, 0)
    masks = jnp.concatenate([mt1, mt2, mt1u, mt2u], axis=1)
    MT[...] = masks
    REP[...] = one_hot(iota((rows, line), 0) // 4 == iota((rows, line), 1))
    MS[...] = nn(REP[...], masks.astype(BF))

    WD[...] = jnp.zeros(WD.shape, BF)
    WD[pl.ds(0, LO), pl.ds(0, LO)] = w_two[0]
    WD[pl.ds(0, LO), pl.ds(128, LO)] = w_two[1]
    WD[pl.ds(128, LO), pl.ds(128, LO)] = w_two[0]
    WD[pl.ds(256, LO), pl.ds(0, LO)] = w_two[2]
    WD[pl.ds(384, LO), pl.ds(0, LO)] = w_two[1]
    WD[pl.ds(384, LO), pl.ds(128, LO)] = w_two[2]
    WI[...] = jnp.zeros(WI.shape, BF)
    for k in range(3):
        for s in range(4):
            WI[pl.ds(128 * k + 16 * s, 16), :] = w_in[k]
    G2[...] = jnp.zeros(G2.shape, F32)
    G2[:, pl.ds(0, LO)] = jnp.broadcast_to(gain2[...].reshape(1, LO), (8, LO))
    U[pl.ds(0, 8), :] = jnp.zeros((8, 768), F32)
    HS[pl.ds(rows, 8), :] = jnp.zeros((8, 512), F32)
    JL[pl.ds(rows, 8), :] = jnp.zeros((8, 3 * HI), F32)

    for i in range(2):
        SRC[pl.ds(128 * i + LO, 128 - LO), :] = jnp.zeros((128 - LO, rows), BF)
    for k in range(6):
        WUP[pl.ds(128 * k + LO, 128 - LO), :] = jnp.zeros((128 - LO, HI), BF)
    load(2)
    to_row = iota((rows, rows), 0)
    from_row = iota((rows, rows), 1)
    perm = one_hot(from_row == ((to_row & 15) // 4) * edge + (to_row // 16) * 4 + (to_row & 3))
    SR[...] = nt(perm, SRC[...]).astype(BF).reshape(nf, 16, 256)
    load(3)

    swap.wait()
    ST[...] = XS[...] + XR[...]
    consts = ST[pl.ds(hr + 64, 16), :]
    col_sum = consts[0:1, :]
    sw = consts[8:9, :]
    stats = ST[pl.ds(0, hr), :]
    mean = stats[:, 64:65] * (1.0 / dd)
    inv = lax.rsqrt(stats[:, 80:81] * (1.0 / dd) - mean * mean + EPS)
    hl = iota((hr, 128), 1)
    pay = jnp.where(hl < 64, inv * (stats - mean * col_sum), jnp.where(hl == 64, inv, 0.0))
    XS[pl.ds(0, hr), :] = pay
    for j in range(4):
        X2[:, j, :] = XS[pl.ds(pl.multiple_of(j * 2 * nf + sec * nf, 8) if nf % 8 == 0 else j * 2 * nf + sec * nf, nf), :]
    to_all(X2, RX, lat_s, lat_r)
    to_all(SR, RW, rew_s, rew_r)
    RX[pl.ds(frm, 1)] = X2[pl.ds(frm, 1)]
    RW[pl.ds(frm, 1)] = SR[pl.ds(frm, 1)]
    all_of(X2, RX, lat_s, lat_r).wait_recv()

    for j in range(4):
        LTS[pl.ds(j, nf, stride=4), :] = RX[:, j, :]
    tl = iota((line, 128), 1)
    lat = jnp.where(tl < 64, LTS[...] + sw, 0.0)
    lat = lat.astype(BF).astype(F32)
    cat = jnp.concatenate(
        [lat, MT[:, 0:128] * pltpu.roll(lat, 1, 0), MT[:, 128:256] * pltpu.roll(lat, 2, 0)], axis=1
    ).astype(BF)
    mine = ((iota((rows, HI), 1) & 127) // 16) == (iota((rows, HI), 0) & 3)
    spread = jnp.where(mine, nn(REP[...], cat), 0.0).astype(BF)
    B[...] = nn(spread, WI[...])
    g1 = gain1[...].reshape(1, HI)

    def act_one(b, carry):
        at = pl.multiple_of(b * RB, RB)
        act = nb(B[pl.ds(at, RB), :], g1, HI)
        ext = jnp.concatenate([carry, act], axis=0)
        m1 = tile(MS[pl.ds(at, RB), 0:128], 3)
        m2 = tile(MS[pl.ds(at, RB), 128:256], 3)
        AC[pl.ds(at, RB), 0:HI] = act.astype(BF)
        AC[pl.ds(at, RB), HI : 2 * HI] = (ext[4 : RB + 4] * m1).astype(BF)
        AC[pl.ds(at, RB), 2 * HI : 3 * HI] = (ext[0:RB] * m2).astype(BF)
        return ext[RB:]

    lax.fori_loop(0, steps, act_one, jnp.zeros((8, HI), F32))
    load(4)
    TR[...] = (B[...] + nn(AC[...], W1[...])).astype(BF)
    U[pl.ds(8, rows), :] = nt(TR[...], WUP[...])
    g2 = G2[0:1, :]

    def act_two(b, carry):
        at = pl.multiple_of(b * RB, RB)
        m1 = tile(MS[pl.ds(at, RB), 0:128], 2)
        m2 = tile(MS[pl.ds(at, RB), 128:256], 2)
        one = U[pl.ds(at, RB + 8), 256:512]
        two = U[pl.ds(at, RB + 8), 512:768]
        up = U[pl.ds(at + 8, RB), 0:256] + one[4 : RB + 4] * m1 + two[0:RB] * m2
        UP[pl.ds(at, RB), :] = up
        act = jnp.concatenate([nb(up[:, :128], g2, LO), nb(up[:, 128:], g2, LO)], axis=1)
        ext = jnp.concatenate([carry, act], axis=0)
        A2[pl.ds(at, RB), 0:256] = act.astype(BF)
        A2[pl.ds(at, RB), 256:512] = (ext[4 : RB + 4] * m1).astype(BF)
        return ext[RB:]

    lax.fori_loop(0, steps, act_two, jnp.zeros((8, 256), F32))
    DEC[...] = (UP[...] + nn(A2[...], WD[...])).astype(BF).reshape(nf, 16, 256)
    to_all(DEC, RD, dec_s, dec_r)
    RD[pl.ds(frm, 1)] = DEC[pl.ds(frm, 1)]

    all_of(SR, RW, rew_s, rew_r).wait_recv()
    HS[pl.ds(0, rows), :] = nt(RW[...].reshape(rows, 256), WD[...])

    def up_grad(b, c):
        at = pl.multiple_of(b * RB, RB)
        m1 = tile(MS[pl.ds(at, RB), 256:384], 2)
        later = HS[pl.ds(at, RB + 8), 256:512]
        second = HS[pl.ds(at, RB), 0:256] + later[4 : RB + 4] * m1
        up = UP[pl.ds(at, RB), :]
        g = RW[pl.ds(b * (RB // 16), RB // 16)].reshape(RB, 256).astype(F32)
        back = [nb_back(second[:, i : i + 128], up[:, i : i + 128], g2, LO) for i in (0, 128)]
        UG[pl.ds(at, RB), :] = (g + jnp.concatenate(back, axis=1)).astype(BF)
        return c

    lax.fori_loop(0, steps, up_grad, 0)
    for k in range(3):
        JL[pl.ds(0, rows), HI * k : HI * k + HI] = nn(UG[...], WUP[pl.ds(256 * k, 256), :])

    def gathered(at):
        m1 = tile(MS[pl.ds(at, RB), 256:384], 3)
        m2 = tile(MS[pl.ds(at, RB), 384:512], 3)
        one = JL[pl.ds(at, RB + 8), HI : 2 * HI]
        two = JL[pl.ds(at, RB + 8), 2 * HI : 3 * HI]
        return JL[pl.ds(at, RB), 0:HI] + one[4 : RB + 4] * m1 + two[8 : RB + 8] * m2

    def trunk_grad(b, c):
        at = pl.multiple_of(b * RB, RB)
        TG[pl.ds(at, RB), :] = gathered(at).astype(BF)
        return c

    lax.fori_loop(0, steps, trunk_grad, 0)
    JL[pl.ds(0, rows), :] = nt(TG[...], W1[...])

    def base_grad(b, c):
        at = pl.multiple_of(b * RB, RB)
        back = nb_back(gathered(at), B[pl.ds(at, RB), :], g1, HI)
        BG[pl.ds(at, RB), :] = (TG[pl.ds(at, RB), :].astype(F32) + back).astype(BF)
        return c

    lax.fori_loop(0, steps, base_grad, 0)
    ZM[...] = jnp.where(mine, nt(BG[...], WI[...]), 0.0).astype(BF)
    rep_t = one_hot(iota((line, rows), 0) == iota((line, rows), 1) // 4)
    y = nn(rep_t, ZM[...])
    lg = y[:, 0:128]
    lg = lg + MT[:, 256:384] * pltpu.roll(y[:, 128:256], line - 1, 0)
    lg = lg + MT[:, 384:512] * pltpu.roll(y[:, 256:384], line - 2, 0)
    lgb = lg.astype(BF)
    lg = lgb.astype(F32)

    pre = LTS[...]
    inv_t = pre[:, 64:65]
    first = jnp.sum(lg * col_sum, axis=-1, keepdims=True) * (1.0 / dd)
    second = jnp.sum(lg * pre, axis=-1, keepdims=True) * (1.0 / dd)
    gram = ST[pl.ds(hr, 64), :]
    gram_hi = gram.astype(BF)
    gram_lo = (gram - gram_hi.astype(F32)).astype(BF)
    quad = nn(lgb[:, 0:64], gram_hi) + nn(lgb[:, 0:64], gram_lo)
    quad = jnp.sum(lg * quad, axis=-1, keepdims=True)
    inv_sq = inv_t * inv_t
    part = inv_sq * (quad - dd * (first * first + second * second * (1.0 + EPS * inv_sq)))
    part = jnp.sum(part, axis=0, keepdims=True)
    PS[...] = jnp.where(
        tl < 64, lg, jnp.where(tl == 64, first, jnp.where(tl == 65, second, jnp.where(tl == 66, part, 0.0)))
    )
    for j in range(4):
        X3[:, j, :] = PS[pl.ds(j, nf, stride=4), :]
    half = RXA.at[sec]
    to_all(X3, half, lg_s, lg_r)
    half[pl.ds(frm, 1)] = X3[pl.ds(frm, 1)]
    all_of(X3, half, lg_s, lg_r).wait_recv()

    trade = pltpu.make_async_remote_copy(
        src_ref=RXA.at[sec], dst_ref=RXA.at[sec], send_sem=sx_s, recv_sem=sx_r,
        device_id=(1 - sec, frm, clip), device_id_type=MESH,
    )
    trade.start()
    trade.wait()
    everyone = jnp.sum(RXA[0, :, 0, :] + RXA[1, :, 0, :], axis=0, keepdims=True)
    ZS[...] = everyone
    for d in above:
        pltpu.make_async_remote_copy(
            src_ref=ZS, dst_ref=ZB.at[clip], send_sem=z_s, recv_sem=z_r,
            device_id=(sec, frm, d), device_id_type=MESH,
        ).start()
    ZB[pl.ds(clip, 1)] = everyone.reshape(1, 1, 128)

    for j in range(4):
        for s in range(2):
            FIN[pl.ds(j * 2 * nf + s * nf, nf), :] = RXA[s, :, j, :]
    got = FIN[...]
    a = got[:, 64:65]
    b = got[:, 65:66]
    stats = ST[pl.ds(0, hr), :]
    mean = stats[:, 64:65] * (1.0 / dd)
    inv = lax.rsqrt(stats[:, 80:81] * (1.0 / dd) - mean * mean + EPS)
    KB[0] = jnp.broadcast_to(inv, (hr, 128))
    KB[1] = jnp.broadcast_to(inv * (inv * b * mean - a), (hr, 128))
    KB[2] = jnp.broadcast_to(inv * inv * b, (hr, 128))
    gotb = got[:, 0:64].astype(BF)

    def token_grad(c, carry):
        at = pl.ds(pl.multiple_of(c * 256, 256), 256)
        grads = nn(gotb, HX[pl.ds(hr, 64), at])
        h = HX[pl.ds(0, hr), at].astype(F32)
        RAW[:, at] = (grads * tile(KB[0], 2) + tile(KB[1], 2) - h * tile(KB[2], 2)).astype(BF)
        return carry

    lax.fori_loop(0, HX.shape[1] // 256, token_grad, 0)
    out_raw = pltpu.make_async_copy(RAW, raw, lsem.at[0])
    out_raw.start()

    all_of(DEC, RD, dec_s, dec_r).wait_recv()
    same = one_hot(iota((256, 256), 0) == iota((256, 256), 1))
    turned = nt(same, RD[...].reshape(rows, 256)).astype(BF)
    perm = one_hot(to_row == ((from_row // edge) * 4) + (lax.rem(from_row, edge) // 4) * 16 + (from_row & 3))
    turned = nn(turned, perm).astype(BF)
    for j in range(4):
        for i in range(2):
            DT[2 * j + i] = turned[128 * i : 128 * i + LO, j * edge : (j + 1) * edge]

    out_dec = pltpu.make_async_copy(DT, dect, lsem.at[1])
    out_dec.start()

    z_all = pltpu.make_async_remote_copy(
        src_ref=ZB.at[pl.ds(0, nc - 1)], dst_ref=ZB.at[pl.ds(0, nc - 1)],
        send_sem=z_s, recv_sem=z_r, device_id=(sec, frm, clip), device_id_type=MESH,
    )
    z_all.wait_recv()
    total = jnp.sum(ZB[:, 0, :], axis=0, keepdims=True)[:, 66:67]
    grow = lax.rsqrt(jnp.maximum(total, 0.0) * (1.0 / count) + EPS)
    scale_out[...] = jnp.broadcast_to(grow, (8, 128))
    out_raw.wait()
    out_dec.wait()

    all_of(X2, RX, lat_s, lat_r).wait_send()
    all_of(SR, RW, rew_s, rew_r).wait_send()
    all_of(DEC, RD, dec_s, dec_r).wait_send()
    all_of(X3, half, lg_s, lg_r).wait_send()
    z_all.wait_send()


def last_kernel(parts, raw, scale, dect, out, decoded, got, done, dec, sems):
    size = got.shape[0] // parts
    inward = pltpu.make_async_copy(dect, dec, sems.at[0])
    outward = pltpu.make_async_copy(dec, decoded, sems.at[0])
    spots = [pl.ds(p * size, size) for p in range(parts)]
    reads = [pltpu.make_async_copy(raw.at[at], got.at[at], sems.at[1 + p]) for p, at in enumerate(spots)]
    for read in reads:
        read.start()
    inward.start()
    writes = []
    for p, at in enumerate(spots):
        reads[p].wait()
        done[at, :] = (got[at, :].astype(F32) * scale[0:1, 0:1]).astype(BF)
        writes.append(pltpu.make_async_copy(done.at[at], out.at[at], sems.at[1 + parts + p]))
        writes[-1].start()
    inward.wait()
    outward.start()
    for write in writes:
        write.wait()
    outward.wait()


def body(nf, nc, dd, count, hidden, modulation, head_w, clip_ids, w_in, gain_one, w_one, w_up, gain_two, w_two, reward_grad):
    wide = hidden.shape[3]
    rows, line, hr = 16 * nf, 4 * nf, 8 * nf
    hid = hidden.reshape(hr, wide)
    hbm = pl.BlockSpec(memory_space=pltpu.HBM)
    vm = pl.BlockSpec(memory_space=pltpu.VMEM)
    dma = pltpu.SemaphoreType.DMA
    V = pltpu.VMEM
    raw, scale, dect = pl.pallas_call(
        functools.partial(main_kernel, nf, nc, dd, count),
        out_shape=(
            jax.ShapeDtypeStruct((hr, wide), BF),
            jax.ShapeDtypeStruct((8, 128), F32),
            jax.ShapeDtypeStruct((8, LO, 4 * nf), BF),
        ),
        in_specs=[hbm, vm, hbm, vm, vm, vm, hbm, hbm, vm, vm, hbm],
        out_specs=(hbm, vm, hbm),
        scratch_shapes=[
            V((hr + 128, wide), BF),
            V((64, wide), BF),
            V((3 * HI, HI), BF),
            V((hr + 80, 128), F32),
            V((hr + 80, 128), F32),
            V((nf, 4, 128), F32),
            V((nf, 4, 128), F32),
            V((256, rows), BF),
            V((nf, 16, 256), BF),
            V((nf, 16, 256), BF),
            V((line, 128), F32),
            V((line, 512), F32),
            V((rows, 512), F32),
            V((rows, line), BF),
            V((512, 256), BF),
            V((HI, HI), BF),
            V((768, HI), BF),
            V((8, 128), F32),
            V((rows, HI), F32),
            V((rows, 3 * HI), BF),
            V((rows, HI), BF),
            V((rows + 8, 768), F32),
            V((rows, 256), F32),
            V((rows, 512), BF),
            V((nf, 16, 256), BF),
            V((rows + 8, 512), F32),
            V((rows, 256), BF),
            V((rows + 8, 3 * HI), F32),
            V((rows, HI), BF),
            V((rows, HI), BF),
            V((rows, HI), BF),
            V((line, 128), F32),
            V((nf, 4, 128), F32),
            V((2, nf, 4, 128), F32),
            V((1, 128), F32),
            V((nc, 1, 128), F32),
            V((hr + 80, 128), F32),
            V((nf, 16, 256), BF),
            V((hr, 128), F32),
            V((3, hr, 128), F32),
            V((hr, wide), BF),
            V((8, LO, 4 * nf), BF),
            dma((20,)),
        ]
        + [dma] * 14,
        compiler_params=pltpu.CompilerParams(
            collective_id=0, has_side_effects=True, vmem_limit_bytes=60 * 1024 * 1024
        ),
        name="exchange",
    )(
        hid, modulation[0], head_w.T, clip_ids, w_in, gain_one, w_one.reshape(3 * HI, HI),
        jnp.transpose(w_up, (0, 2, 1)), gain_two, w_two, jnp.transpose(reward_grad[0], (0, 2, 1)),
    )
    parts = min(4, hr // 16)
    grad, dect = pl.pallas_call(
        functools.partial(last_kernel, parts),
        out_shape=(
            jax.ShapeDtypeStruct((hr, wide), BF),
            jax.ShapeDtypeStruct((8, LO, 4 * nf), BF),
        ),
        in_specs=[pl.BlockSpec(memory_space=pl.ANY), vm, pl.BlockSpec(memory_space=pl.ANY)],
        out_specs=(hbm, hbm),
        scratch_shapes=[V((hr, wide), BF), V((hr, wide), BF), V((8, LO, 4 * nf), BF), dma((1 + 2 * parts,))],
        compiler_params=pltpu.CompilerParams(vmem_limit_bytes=60 * 1024 * 1024),
        name="finish",
    )(raw, scale, dect)
    return jnp.transpose(dect, (0, 2, 1))[None], grad.reshape(hidden.shape)


def solution(mesh):
    nf, nc = mesh.shape["frm"], mesh.shape["clip"]

    def whole(hidden, *rest):
        dd = hidden.shape[3]
        count = float(hidden.size)
        in_specs = (
            P("clip", "frm", None, "sec"),
            P("clip", None, "sec"),
            P("sec", None),
            P("clip", None),
            P(),
            P(),
            P(),
            P(),
            P(),
            P(),
            P("clip", "frm", "sec", None),
        )
        out_specs = (P("clip", "frm", "sec", None), P("clip", "frm", None, "sec"))
        return jax.shard_map(
            functools.partial(body, nf, nc, dd, count),
            mesh=mesh, in_specs=in_specs, out_specs=out_specs, check_vma=False,
        )(hidden, *rest)

    return whole
```

```python
import functools

import jax
import jax.numpy as jnp
from jax import lax
from jax.experimental import pallas as pl
from jax.experimental.pallas import tpu as pltpu
from jax.sharding import PartitionSpec as P

BF = jnp.bfloat16
F32 = jnp.float32
MESH = pl.DeviceIdType.MESH
HI = 384
LO = 96
EPS = 1e-6
RB = 64


def nn(a, b):
    return jnp.dot(a, b, preferred_element_type=F32)


def nt(a, b):
    return lax.dot_general(a, b, (((1,), (1,)), ((), ())), preferred_element_type=F32)


def iota(shape, dim):
    return lax.broadcasted_iota(jnp.int32, shape, dim)


def one_hot(cond):
    return jnp.where(cond, 1.0, 0.0).astype(BF)


def sigmoid(x):
    return 0.5 * jnp.tanh(0.5 * x) + 0.5


def tile(mask, times):
    return jnp.concatenate([mask] * times, axis=1)


def nb(x, gain, width):
    r = lax.rsqrt(jnp.sum(x * x, axis=-1, keepdims=True) * (1.0 / width) + EPS)
    n = x * r * gain
    return n * sigmoid(n)


def nb_back(g, x, gain, width):
    r = lax.rsqrt(jnp.sum(x * x, axis=-1, keepdims=True) * (1.0 / width) + EPS)
    n = x * r * gain
    sg = sigmoid(n)
    u = g * sg * (1.0 + n * (1.0 - sg)) * gain
    mixed = jnp.sum(u * x, axis=-1, keepdims=True) * (1.0 / width)
    return r * u - x * (r * r * r * mixed)


def main_kernel(
    nf, nc, dd, count,
    hidden, mod_h, head_w, ids_h, w_in_h, gain1_h, w_one, w_up, gain2_h, w_two_h, reward,
    raw, scale_out, dect,
    HX, HW, W1, XS, XR, X2, RX, SRC, SR, RW, LTS, MT, MS, REP, WD, WI, WUP, G2,
    B, AC, TR, U, UP, A2, DEC, HS, UG, JL, TG, BG, ZM, PS, X3, RXA, ZS, ZB, ST, RD, FIN, KB, RAW, DT, mod, ids, w_in, gain1, gain2, w_two, SC,
    lsem, sec_s, sec_r, lat_s, lat_r, rew_s, rew_r, dec_s, dec_r, lg_s, lg_r, sx_s, sx_r, z_s, z_r,
):
    sec = lax.axis_index("sec")
    frm = lax.axis_index("frm")
    clip = lax.axis_index("clip")
    rows = 16 * nf
    line = 4 * nf
    hr = 8 * nf
    steps = rows // RB

    edge = 4 * nf
    loads = [
        [pltpu.make_async_copy(head_w, HW, lsem.at[0]), pltpu.make_async_copy(mod_h, mod, lsem.at[20])],
        [pltpu.make_async_copy(hidden, HX.at[pl.ds(0, hr)], lsem.at[1])],
        [
            pltpu.make_async_copy(
                reward.at[2 * j + i], SRC.at[pl.ds(128 * i, LO), pl.ds(j * edge, edge)], lsem.at[6 + 2 * j + i]
            )
            for j in range(4) for i in range(2)
        ],
        [
            pltpu.make_async_copy(
                w_up.at[k, pl.ds(LO * i, LO)], WUP.at[pl.ds(256 * k + 128 * i, LO)], lsem.at[14 + 2 * k + i]
            )
            for k in range(3) for i in range(2)
        ],
        [pltpu.make_async_copy(w_one, W1, lsem.at[4])],
        [
            pltpu.make_async_copy(src, dst, lsem.at[21 + i])
            for i, (src, dst) in enumerate(
                ((ids_h, ids), (w_in_h, w_in), (gain1_h, gain1), (gain2_h, gain2), (w_two_h, w_two))
            )
        ],
    ]

    def load(which):
        for copy in loads[which]:
            copy.wait()

    for group in loads[:2]:
        for copy in group:
            copy.start()

    nx = 4
    ny = nf // nx
    yy, xx = frm // nx, lax.rem(frm, nx)
    far = sorted(
        ((min(dy, ny - dy) + min(dx, nx - dx), dy, dx) for dy in range(ny) for dx in range(nx) if dy or dx),
        reverse=True,
    )
    peers = [lax.rem(yy + dy, ny) * nx + lax.rem(xx + dx, nx) for _, dy, dx in far]
    above = [lax.rem(clip + dz, nc) for dz in sorted(range(1, nc), key=lambda dz: -min(dz, nc - dz))]

    barrier = pltpu.get_barrier_semaphore()
    for d in peers:
        pl.semaphore_signal(barrier, inc=1, device_id=(sec, d, clip), device_id_type=MESH)
    for d in above:
        pl.semaphore_signal(barrier, inc=1, device_id=(sec, frm, d), device_id_type=MESH)
    pl.semaphore_signal(barrier, inc=1, device_id=(1 - sec, frm, clip), device_id_type=MESH)
    for group in loads[2:]:
        for copy in group:
            copy.start()

    def to_all(src, dst, ssem, rsem):
        for d in peers:
            pltpu.make_async_remote_copy(
                src_ref=src.at[d], dst_ref=dst.at[frm], send_sem=ssem, recv_sem=rsem,
                device_id=(sec, d, clip), device_id_type=MESH,
            ).start()

    def all_of(src, dst, ssem, rsem):
        return pltpu.make_async_remote_copy(
            src_ref=src.at[pl.ds(0, nf - 1)], dst_ref=dst.at[pl.ds(0, nf - 1)],
            send_sem=ssem, recv_sem=rsem, device_id=(sec, frm, clip), device_id_type=MESH,
        )

    HX[pl.ds(hr + 64, 16), :] = jnp.ones((16, HX.shape[1]), BF)
    HX[pl.ds(hr + 80, 48), :] = jnp.zeros((48, HX.shape[1]), BF)
    load(0)
    shift = mod[0:1, :]
    HX[pl.ds(hr, 64), :] = (HW[...].astype(F32) * (1.0 + mod[1:2, :])).astype(BF)
    coarse = shift.astype(BF).astype(F32)
    pick = iota((16, HX.shape[1]), 0)
    pair = jnp.where(pick == 0, coarse, jnp.where(pick == 1, shift - coarse, 0.0)).astype(BF)
    shifted = nt(pair, HW[...])
    XS[pl.ds(hr, 80), :] = nt(HX[pl.ds(hr, 80), :], HX[pl.ds(hr, 128), :])
    XS[pl.ds(hr + 72, 8), pl.ds(0, 64)] = jnp.broadcast_to(shifted[0:1, :] + shifted[1:2, :], (8, 64))

    load(1)
    block = min(hr, 64)
    for b in range(hr // block):
        h = HX[pl.ds(b * block, block), :]
        x = h.astype(F32)
        total = jnp.sum(x * x, axis=-1, keepdims=True)
        XS[pl.ds(b * block, block), :] = nt(h, HX[pl.ds(hr, 128), :]) + jnp.where(
            iota((block, 128), 1) == 80, total, 0.0
        )

    pl.semaphore_wait(barrier, nf - 1 + nc)
    swap = pltpu.make_async_remote_copy(
        src_ref=XS, dst_ref=XR, send_sem=sec_s, recv_sem=sec_r,
        device_id=(1 - sec, frm, clip), device_id_type=MESH,
    )
    swap.start()

    load(5)
    when = iota((line, 128), 0)
    own = jnp.broadcast_to(ids[...].astype(F32), (128, line)).T
    mt1 = jnp.where((own == pltpu.roll(own, 1, 0)) & (when >= 1), 1.0, 0.0)
    mt2 = jnp.where((own == pltpu.roll(own, 2, 0)) & (when >= 2), 1.0, 0.0)
    mt1u = pltpu.roll(mt1, line - 1, 0)
    mt2u = pltpu.roll(mt2, line - 2, 0)
    masks = jnp.concatenate([mt1, mt2, mt1u, mt2u], axis=1)
    MT[...] = masks
    REP[...] = one_hot(iota((rows, line), 0) // 4 == iota((rows, line), 1))
    MS[...] = nn(REP[...], masks.astype(BF))

    WD[...] = jnp.zeros(WD.shape, BF)
    WD[pl.ds(0, LO), pl.ds(0, LO)] = w_two[0]
    WD[pl.ds(0, LO), pl.ds(128, LO)] = w_two[1]
    WD[pl.ds(128, LO), pl.ds(128, LO)] = w_two[0]
    WD[pl.ds(256, LO), pl.ds(0, LO)] = w_two[2]
    WD[pl.ds(384, LO), pl.ds(0, LO)] = w_two[1]
    WD[pl.ds(384, LO), pl.ds(128, LO)] = w_two[2]
    WI[...] = jnp.zeros(WI.shape, BF)
    for k in range(3):
        for s in range(4):
            WI[pl.ds(128 * k + 16 * s, 16), :] = w_in[k]
    G2[...] = jnp.zeros(G2.shape, F32)
    G2[:, pl.ds(0, LO)] = jnp.broadcast_to(gain2[...].reshape(1, LO), (8, LO))
    U[pl.ds(0, 8), :] = jnp.zeros((8, 768), F32)
    HS[pl.ds(rows, 8), :] = jnp.zeros((8, 512), F32)
    JL[pl.ds(rows, 8), :] = jnp.zeros((8, 3 * HI), F32)

    for i in range(2):
        SRC[pl.ds(128 * i + LO, 128 - LO), :] = jnp.zeros((128 - LO, rows), BF)
    for k in range(6):
        WUP[pl.ds(128 * k + LO, 128 - LO), :] = jnp.zeros((128 - LO, HI), BF)
    load(2)
    to_row = iota((rows, rows), 0)
    from_row = iota((rows, rows), 1)
    perm = one_hot(from_row == ((to_row & 15) // 4) * edge + (to_row // 16) * 4 + (to_row & 3))
    SR[...] = nt(perm, SRC[...]).astype(BF).reshape(nf, 16, 256)
    load(3)

    swap.wait()
    ST[...] = XS[...] + XR[...]
    consts = ST[pl.ds(hr + 64, 16), :]
    col_sum = consts[0:1, :]
    sw = consts[8:9, :]
    stats = ST[pl.ds(0, hr), :]
    mean = stats[:, 64:65] * (1.0 / dd)
    inv = lax.rsqrt(stats[:, 80:81] * (1.0 / dd) - mean * mean + EPS)
    hl = iota((hr, 128), 1)
    pay = jnp.where(hl < 64, inv * (stats - mean * col_sum), jnp.where(hl == 64, inv, 0.0))
    XS[pl.ds(0, hr), :] = pay
    for j in range(4):
        X2[:, j, :] = XS[pl.ds(pl.multiple_of(j * 2 * nf + sec * nf, 8) if nf % 8 == 0 else j * 2 * nf + sec * nf, nf), :]
    to_all(X2, RX, lat_s, lat_r)
    to_all(SR, RW, rew_s, rew_r)
    RX[pl.ds(frm, 1)] = X2[pl.ds(frm, 1)]
    RW[pl.ds(frm, 1)] = SR[pl.ds(frm, 1)]
    all_of(X2, RX, lat_s, lat_r).wait_recv()

    for j in range(4):
        LTS[pl.ds(j, nf, stride=4), :] = RX[:, j, :]
    tl = iota((line, 128), 1)
    lat = jnp.where(tl < 64, LTS[...] + sw, 0.0)
    lat = lat.astype(BF).astype(F32)
    cat = jnp.concatenate(
        [lat, MT[:, 0:128] * pltpu.roll(lat, 1, 0), MT[:, 128:256] * pltpu.roll(lat, 2, 0)], axis=1
    ).astype(BF)
    mine = ((iota((rows, HI), 1) & 127) // 16) == (iota((rows, HI), 0) & 3)
    spread = jnp.where(mine, nn(REP[...], cat), 0.0).astype(BF)
    B[...] = nn(spread, WI[...])
    g1 = gain1[...].reshape(1, HI)

    def act_one(b, carry):
        at = pl.multiple_of(b * RB, RB)
        act = nb(B[pl.ds(at, RB), :], g1, HI)
        ext = jnp.concatenate([carry, act], axis=0)
        m1 = tile(MS[pl.ds(at, RB), 0:128], 3)
        m2 = tile(MS[pl.ds(at, RB), 128:256], 3)
        AC[pl.ds(at, RB), 0:HI] = act.astype(BF)
        AC[pl.ds(at, RB), HI : 2 * HI] = (ext[4 : RB + 4] * m1).astype(BF)
        AC[pl.ds(at, RB), 2 * HI : 3 * HI] = (ext[0:RB] * m2).astype(BF)
        return ext[RB:]

    lax.fori_loop(0, steps, act_one, jnp.zeros((8, HI), F32), unroll=True)
    load(4)
    TR[...] = (B[...] + nn(AC[...], W1[...])).astype(BF)
    U[pl.ds(8, rows), :] = nt(TR[...], WUP[...])
    g2 = G2[0:1, :]

    def act_two(b, carry):
        at = pl.multiple_of(b * RB, RB)
        m1 = tile(MS[pl.ds(at, RB), 0:128], 2)
        m2 = tile(MS[pl.ds(at, RB), 128:256], 2)
        one = U[pl.ds(at, RB + 8), 256:512]
        two = U[pl.ds(at, RB + 8), 512:768]
        up = U[pl.ds(at + 8, RB), 0:256] + one[4 : RB + 4] * m1 + two[0:RB] * m2
        UP[pl.ds(at, RB), :] = up
        act = jnp.concatenate([nb(up[:, :128], g2, LO), nb(up[:, 128:], g2, LO)], axis=1)
        ext = jnp.concatenate([carry, act], axis=0)
        A2[pl.ds(at, RB), 0:256] = act.astype(BF)
        A2[pl.ds(at, RB), 256:512] = (ext[4 : RB + 4] * m1).astype(BF)
        return ext[RB:]

    lax.fori_loop(0, steps, act_two, jnp.zeros((8, 256), F32), unroll=True)
    DEC[...] = (UP[...] + nn(A2[...], WD[...])).astype(BF).reshape(nf, 16, 256)
    to_all(DEC, RD, dec_s, dec_r)
    RD[pl.ds(frm, 1)] = DEC[pl.ds(frm, 1)]

    all_of(SR, RW, rew_s, rew_r).wait_recv()
    HS[pl.ds(0, rows), :] = nt(RW[...].reshape(rows, 256), WD[...])

    def up_grad(b, c):
        at = pl.multiple_of(b * RB, RB)
        m1 = tile(MS[pl.ds(at, RB), 256:384], 2)
        later = HS[pl.ds(at, RB + 8), 256:512]
        second = HS[pl.ds(at, RB), 0:256] + later[4 : RB + 4] * m1
        up = UP[pl.ds(at, RB), :]
        g = RW[pl.ds(b * (RB // 16), RB // 16)].reshape(RB, 256).astype(F32)
        back = [nb_back(second[:, i : i + 128], up[:, i : i + 128], g2, LO) for i in (0, 128)]
        UG[pl.ds(at, RB), :] = (g + jnp.concatenate(back, axis=1)).astype(BF)
        return c

    lax.fori_loop(0, steps, up_grad, 0, unroll=True)
    for k in range(3):
        JL[pl.ds(0, rows), HI * k : HI * k + HI] = nn(UG[...], WUP[pl.ds(256 * k, 256), :])

    def gathered(at):
        m1 = tile(MS[pl.ds(at, RB), 256:384], 3)
        m2 = tile(MS[pl.ds(at, RB), 384:512], 3)
        one = JL[pl.ds(at, RB + 8), HI : 2 * HI]
        two = JL[pl.ds(at, RB + 8), 2 * HI : 3 * HI]
        return JL[pl.ds(at, RB), 0:HI] + one[4 : RB + 4] * m1 + two[8 : RB + 8] * m2

    def trunk_grad(b, c):
        at = pl.multiple_of(b * RB, RB)
        TG[pl.ds(at, RB), :] = gathered(at).astype(BF)
        return c

    lax.fori_loop(0, steps, trunk_grad, 0, unroll=True)
    JL[pl.ds(0, rows), :] = nt(TG[...], W1[...])

    def base_grad(b, c):
        at = pl.multiple_of(b * RB, RB)
        back = nb_back(gathered(at), B[pl.ds(at, RB), :], g1, HI)
        BG[pl.ds(at, RB), :] = (TG[pl.ds(at, RB), :].astype(F32) + back).astype(BF)
        return c

    lax.fori_loop(0, steps, base_grad, 0, unroll=True)
    ZM[...] = jnp.where(mine, nt(BG[...], WI[...]), 0.0).astype(BF)
    rep_t = one_hot(iota((line, rows), 0) == iota((line, rows), 1) // 4)
    y = nn(rep_t, ZM[...])
    lg = y[:, 0:128]
    lg = lg + MT[:, 256:384] * pltpu.roll(y[:, 128:256], line - 1, 0)
    lg = lg + MT[:, 384:512] * pltpu.roll(y[:, 256:384], line - 2, 0)
    lgb = lg.astype(BF)
    lg = lgb.astype(F32)

    pre = LTS[...]
    inv_t = pre[:, 64:65]
    first = jnp.sum(lg * col_sum, axis=-1, keepdims=True) * (1.0 / dd)
    second = jnp.sum(lg * pre, axis=-1, keepdims=True) * (1.0 / dd)
    gram = ST[pl.ds(hr, 64), :]
    gram_hi = gram.astype(BF)
    gram_lo = (gram - gram_hi.astype(F32)).astype(BF)
    quad = nn(lgb[:, 0:64], gram_hi) + nn(lgb[:, 0:64], gram_lo)
    quad = jnp.sum(lg * quad, axis=-1, keepdims=True)
    inv_sq = inv_t * inv_t
    part = inv_sq * (quad - dd * (first * first + second * second * (1.0 + EPS * inv_sq)))
    part = jnp.sum(part, axis=0, keepdims=True)
    PS[...] = jnp.where(
        tl < 64, lg, jnp.where(tl == 64, first, jnp.where(tl == 65, second, jnp.where(tl == 66, part, 0.0)))
    )
    for j in range(4):
        X3[:, j, :] = PS[pl.ds(j, nf, stride=4), :]
    half = RXA.at[sec]
    to_all(X3, half, lg_s, lg_r)
    half[pl.ds(frm, 1)] = X3[pl.ds(frm, 1)]
    all_of(X3, half, lg_s, lg_r).wait_recv()

    trade = pltpu.make_async_remote_copy(
        src_ref=RXA.at[sec], dst_ref=RXA.at[sec], send_sem=sx_s, recv_sem=sx_r,
        device_id=(1 - sec, frm, clip), device_id_type=MESH,
    )
    trade.start()
    trade.wait()
    everyone = jnp.sum(RXA[0, :, 0, :] + RXA[1, :, 0, :], axis=0, keepdims=True)
    ZS[...] = everyone
    for d in above:
        pltpu.make_async_remote_copy(
            src_ref=ZS, dst_ref=ZB.at[clip], send_sem=z_s, recv_sem=z_r,
            device_id=(sec, frm, d), device_id_type=MESH,
        ).start()
    ZB[pl.ds(clip, 1)] = everyone.reshape(1, 1, 128)

    for j in range(4):
        for s in range(2):
            FIN[pl.ds(j * 2 * nf + s * nf, nf), :] = RXA[s, :, j, :]
    got = FIN[...]
    a = got[:, 64:65]
    b = got[:, 65:66]
    stats = ST[pl.ds(0, hr), :]
    mean = stats[:, 64:65] * (1.0 / dd)
    inv = lax.rsqrt(stats[:, 80:81] * (1.0 / dd) - mean * mean + EPS)
    KB[0] = jnp.broadcast_to(inv, (hr, 128))
    KB[1] = jnp.broadcast_to(inv * (inv * b * mean - a), (hr, 128))
    KB[2] = jnp.broadcast_to(inv * inv * b, (hr, 128))
    gotb = got[:, 0:64].astype(BF)

    def token_grad(c, carry):
        at = pl.ds(pl.multiple_of(c * 256, 256), 256)
        grads = nn(gotb, HX[pl.ds(hr, 64), at])
        h = HX[pl.ds(0, hr), at].astype(F32)
        RAW[:, at] = (grads * tile(KB[0], 2) + tile(KB[1], 2) - h * tile(KB[2], 2)).astype(BF)
        return carry

    lax.fori_loop(0, HX.shape[1] // 256, token_grad, 0, unroll=2)
    out_raw = pltpu.make_async_copy(RAW, raw, lsem.at[0])
    out_raw.start()

    all_of(DEC, RD, dec_s, dec_r).wait_recv()
    same = one_hot(iota((256, 256), 0) == iota((256, 256), 1))
    turned = nt(same, RD[...].reshape(rows, 256)).astype(BF)
    perm = one_hot(to_row == ((from_row // edge) * 4) + (lax.rem(from_row, edge) // 4) * 16 + (from_row & 3))
    turned = nn(turned, perm).astype(BF)
    for j in range(4):
        for i in range(2):
            DT[2 * j + i] = turned[128 * i : 128 * i + LO, j * edge : (j + 1) * edge]

    out_dec = pltpu.make_async_copy(DT, dect, lsem.at[1])
    out_dec.start()

    z_all = pltpu.make_async_remote_copy(
        src_ref=ZB.at[pl.ds(0, nc - 1)], dst_ref=ZB.at[pl.ds(0, nc - 1)],
        send_sem=z_s, recv_sem=z_r, device_id=(sec, frm, clip), device_id_type=MESH,
    )
    z_all.wait_recv()
    total = jnp.sum(ZB[:, 0, :], axis=0, keepdims=True)[:, 66:67]
    grow = lax.rsqrt(jnp.maximum(total, 0.0) * (1.0 / count) + EPS)
    SC[...] = jnp.broadcast_to(grow, (8, 128))
    out_scale = pltpu.make_async_copy(SC, scale_out, lsem.at[2])
    out_scale.start()
    out_scale.wait()
    out_raw.wait()
    out_dec.wait()

    all_of(X2, RX, lat_s, lat_r).wait_send()
    all_of(SR, RW, rew_s, rew_r).wait_send()
    all_of(DEC, RD, dec_s, dec_r).wait_send()
    all_of(X3, half, lg_s, lg_r).wait_send()
    z_all.wait_send()


def last_kernel(parts, raw, scale_h, dect, out, decoded, got, done, dec, scale, sems):
    factor = pltpu.make_async_copy(scale_h, scale, sems.at[1 + 2 * parts])
    factor.start()
    size = got.shape[0] // parts
    inward = pltpu.make_async_copy(dect, dec, sems.at[0])
    outward = pltpu.make_async_copy(dec, decoded, sems.at[0])
    spots = [pl.ds(p * size, size) for p in range(parts)]
    reads = [pltpu.make_async_copy(raw.at[at], got.at[at], sems.at[1 + p]) for p, at in enumerate(spots)]
    for read in reads:
        read.start()
    inward.start()
    factor.wait()
    writes = []
    for p, at in enumerate(spots):
        reads[p].wait()
        done[at, :] = (got[at, :].astype(F32) * scale[0:1, 0:1]).astype(BF)
        writes.append(pltpu.make_async_copy(done.at[at], out.at[at], sems.at[1 + parts + p]))
        writes[-1].start()
    inward.wait()
    outward.start()
    for write in writes:
        write.wait()
    outward.wait()


def body(nf, nc, dd, count, hidden, modulation, head_w, clip_ids, w_in, gain_one, w_one, w_up, gain_two, w_two, reward_grad):
    wide = hidden.shape[3]
    rows, line, hr = 16 * nf, 4 * nf, 8 * nf
    hid = hidden.reshape(hr, wide)
    hbm = pl.BlockSpec(memory_space=pltpu.HBM)
    dma = pltpu.SemaphoreType.DMA
    V = pltpu.VMEM
    raw, scale, dect = pl.pallas_call(
        functools.partial(main_kernel, nf, nc, dd, count),
        out_shape=(
            jax.ShapeDtypeStruct((hr, wide), BF),
            jax.ShapeDtypeStruct((8, 128), F32),
            jax.ShapeDtypeStruct((8, LO, 4 * nf), BF),
        ),
        in_specs=[hbm] * 11,
        out_specs=(hbm, hbm, hbm),
        scratch_shapes=[
            V((hr + 128, wide), BF),
            V((64, wide), BF),
            V((3 * HI, HI), BF),
            V((hr + 80, 128), F32),
            V((hr + 80, 128), F32),
            V((nf, 4, 128), F32),
            V((nf, 4, 128), F32),
            V((256, rows), BF),
            V((nf, 16, 256), BF),
            V((nf, 16, 256), BF),
            V((line, 128), F32),
            V((line, 512), F32),
            V((rows, 512), F32),
            V((rows, line), BF),
            V((512, 256), BF),
            V((HI, HI), BF),
            V((768, HI), BF),
            V((8, 128), F32),
            V((rows, HI), F32),
            V((rows, 3 * HI), BF),
            V((rows, HI), BF),
            V((rows + 8, 768), F32),
            V((rows, 256), F32),
            V((rows, 512), BF),
            V((nf, 16, 256), BF),
            V((rows + 8, 512), F32),
            V((rows, 256), BF),
            V((rows + 8, 3 * HI), F32),
            V((rows, HI), BF),
            V((rows, HI), BF),
            V((rows, HI), BF),
            V((line, 128), F32),
            V((nf, 4, 128), F32),
            V((2, nf, 4, 128), F32),
            V((1, 128), F32),
            V((nc, 1, 128), F32),
            V((hr + 80, 128), F32),
            V((nf, 16, 256), BF),
            V((hr, 128), F32),
            V((3, hr, 128), F32),
            V((hr, wide), BF),
            V((8, LO, 4 * nf), BF),
            V((2, wide), F32),
            V((1, line), jnp.int32),
            V((3, 16, HI), BF),
            V((HI,), F32),
            V((LO,), F32),
            V((3, LO, LO), BF),
            V((8, 128), F32),
            dma((26,)),
        ]
        + [dma] * 14,
        compiler_params=pltpu.CompilerParams(
            collective_id=0, has_side_effects=True, vmem_limit_bytes=60 * 1024 * 1024
        ),
        name="exchange",
    )(
        hid, modulation[0], head_w.T, clip_ids, w_in, gain_one, w_one.reshape(3 * HI, HI),
        jnp.transpose(w_up, (0, 2, 1)), gain_two, w_two, jnp.transpose(reward_grad[0], (0, 2, 1)),
    )
    parts = min(4, hr // 16)
    grad, dect = pl.pallas_call(
        functools.partial(last_kernel, parts),
        out_shape=(
            jax.ShapeDtypeStruct((hr, wide), BF),
            jax.ShapeDtypeStruct((8, LO, 4 * nf), BF),
        ),
        in_specs=[hbm, hbm, hbm],
        out_specs=(hbm, hbm),
        scratch_shapes=[V((hr, wide), BF), V((hr, wide), BF), V((8, LO, 4 * nf), BF), V((8, 128), F32), dma((2 + 2 * parts,))],
        compiler_params=pltpu.CompilerParams(vmem_limit_bytes=60 * 1024 * 1024),
        name="finish",
    )(raw, scale, dect)
    return jnp.transpose(dect, (0, 2, 1))[None], grad.reshape(hidden.shape)


def solution(mesh):
    nf, nc = mesh.shape["frm"], mesh.shape["clip"]

    def whole(hidden, *rest):
        dd = hidden.shape[3]
        count = float(hidden.size)
        in_specs = (
            P("clip", "frm", None, "sec"),
            P("clip", None, "sec"),
            P("sec", None),
            P("clip", None),
            P(),
            P(),
            P(),
            P(),
            P(),
            P(),
            P("clip", "frm", "sec", None),
        )
        out_specs = (P("clip", "frm", "sec", None), P("clip", "frm", None, "sec"))
        return jax.shard_map(
            functools.partial(body, nf, nc, dd, count),
            mesh=mesh, in_specs=in_specs, out_specs=out_specs, check_vma=False,
        )(hidden, *rest)

    return whole
```

```python
import functools

import jax
import jax.numpy as jnp
from jax import lax
from jax.experimental import pallas as pl
from jax.experimental.pallas import tpu as pltpu
from jax.sharding import PartitionSpec as P

BF = jnp.bfloat16
F32 = jnp.float32
MESH = pl.DeviceIdType.MESH
HI = 384
LO = 96
EPS = 1e-6
RB = 64


def nn(a, b):
    return jnp.dot(a, b, preferred_element_type=F32)


def nt(a, b):
    return lax.dot_general(a, b, (((1,), (1,)), ((), ())), preferred_element_type=F32)


def iota(shape, dim):
    return lax.broadcasted_iota(jnp.int32, shape, dim)


def one_hot(cond):
    return jnp.where(cond, 1.0, 0.0).astype(BF)


def sigmoid(x):
    return 0.5 * jnp.tanh(0.5 * x) + 0.5


def tile(mask, times):
    return jnp.concatenate([mask] * times, axis=1)


def nb(x, gain, width):
    r = lax.rsqrt(jnp.sum(x * x, axis=-1, keepdims=True) * (1.0 / width) + EPS)
    n = x * r * gain
    return n * sigmoid(n)


def nb_back(g, x, gain, width):
    r = lax.rsqrt(jnp.sum(x * x, axis=-1, keepdims=True) * (1.0 / width) + EPS)
    n = x * r * gain
    sg = sigmoid(n)
    u = g * sg * (1.0 + n * (1.0 - sg)) * gain
    mixed = jnp.sum(u * x, axis=-1, keepdims=True) * (1.0 / width)
    return r * u - x * (r * r * r * mixed)


def main_kernel(
    nf, nc, dd, count,
    hidden, mod_h, head_w, ids_h, w_in_h, gain1_h, w_one, w_up, gain2_h, w_two_h, reward,
    raw, scale_out, dect,
    HX, HW, W1, XS, XR, X2, RX, SRC, SR, RW, LTS, MT, MS, REP, WD, WI, WUP, G2,
    B, AC, TR, U, UP, A2, DEC, HS, UG, JL, TG, BG, ZM, PS, X3, RXA, ZS, ZB, ST, RD, FIN, KB, RAW, DT, mod, ids, w_in, gain1, gain2, w_two, SC,
    lsem, sec_s, sec_r, lat_s, lat_r, rew_s, rew_r, dec_s, dec_r, lg_s, lg_r, sx_s, sx_r, z_s, z_r,
):
    sec = lax.axis_index("sec")
    frm = lax.axis_index("frm")
    clip = lax.axis_index("clip")
    rows = 16 * nf
    line = 4 * nf
    hr = 8 * nf
    steps = rows // RB

    edge = 4 * nf
    loads = [
        [pltpu.make_async_copy(head_w, HW, lsem.at[0]), pltpu.make_async_copy(mod_h, mod, lsem.at[20])],
        [pltpu.make_async_copy(hidden, HX.at[pl.ds(0, hr)], lsem.at[1])],
        [
            pltpu.make_async_copy(
                reward.at[2 * j + i], SRC.at[pl.ds(128 * i, LO), pl.ds(j * edge, edge)], lsem.at[6 + 2 * j + i]
            )
            for j in range(4) for i in range(2)
        ],
        [
            pltpu.make_async_copy(
                w_up.at[k, pl.ds(LO * i, LO)], WUP.at[pl.ds(256 * k + 128 * i, LO)], lsem.at[14 + 2 * k + i]
            )
            for k in range(3) for i in range(2)
        ],
        [pltpu.make_async_copy(w_one, W1, lsem.at[4])],
        [
            pltpu.make_async_copy(src, dst, lsem.at[21 + i])
            for i, (src, dst) in enumerate(
                ((ids_h, ids), (w_in_h, w_in), (gain1_h, gain1), (gain2_h, gain2), (w_two_h, w_two))
            )
        ],
    ]

    def load(which):
        for copy in loads[which]:
            copy.wait()

    for group in loads[:2]:
        for copy in group:
            copy.start()

    nx = 4
    ny = nf // nx
    yy, xx = frm // nx, lax.rem(frm, nx)
    ways = [(min(dy, ny - dy) + min(dx, nx - dx), dy, dx) for dy in range(ny) for dx in range(nx) if dy or dx]
    seen = {}
    far = []
    for hop, dy, dx in sorted(ways, reverse=True):
        side = (hop, 2 * dy > ny)
        seen[side] = seen.get(side, 0) + 1
        far.append((-hop, seen[side], dy, dx))
    far = [(-hop, dy, dx) for hop, _, dy, dx in sorted(far)]
    peers = [lax.rem(yy + dy, ny) * nx + lax.rem(xx + dx, nx) for _, dy, dx in far]
    above = [lax.rem(clip + dz, nc) for dz in sorted(range(1, nc), key=lambda dz: -min(dz, nc - dz))]

    barrier = pltpu.get_barrier_semaphore()
    for d in peers:
        pl.semaphore_signal(barrier, inc=1, device_id=(sec, d, clip), device_id_type=MESH)
    for d in above:
        pl.semaphore_signal(barrier, inc=1, device_id=(sec, frm, d), device_id_type=MESH)
    pl.semaphore_signal(barrier, inc=1, device_id=(1 - sec, frm, clip), device_id_type=MESH)
    for group in loads[2:]:
        for copy in group:
            copy.start()

    def to_all(src, dst, ssem, rsem, some=slice(None)):
        for d in peers[some]:
            pltpu.make_async_remote_copy(
                src_ref=src.at[d], dst_ref=dst.at[frm], send_sem=ssem, recv_sem=rsem,
                device_id=(sec, d, clip), device_id_type=MESH,
            ).start()

    def all_of(src, dst, ssem, rsem):
        return pltpu.make_async_remote_copy(
            src_ref=src.at[pl.ds(0, nf - 1)], dst_ref=dst.at[pl.ds(0, nf - 1)],
            send_sem=ssem, recv_sem=rsem, device_id=(sec, frm, clip), device_id_type=MESH,
        )

    HX[pl.ds(hr + 64, 16), :] = jnp.ones((16, HX.shape[1]), BF)
    HX[pl.ds(hr + 80, 48), :] = jnp.zeros((48, HX.shape[1]), BF)
    load(0)
    shift = mod[0:1, :]
    HX[pl.ds(hr, 64), :] = (HW[...].astype(F32) * (1.0 + mod[1:2, :])).astype(BF)
    coarse = shift.astype(BF).astype(F32)
    pick = iota((16, HX.shape[1]), 0)
    pair = jnp.where(pick == 0, coarse, jnp.where(pick == 1, shift - coarse, 0.0)).astype(BF)
    shifted = nt(pair, HW[...])
    XS[pl.ds(hr, 80), :] = nt(HX[pl.ds(hr, 80), :], HX[pl.ds(hr, 128), :])
    XS[pl.ds(hr + 72, 8), pl.ds(0, 64)] = jnp.broadcast_to(shifted[0:1, :] + shifted[1:2, :], (8, 64))

    load(1)
    block = min(hr, 64)
    for b in range(hr // block):
        h = HX[pl.ds(b * block, block), :]
        x = h.astype(F32)
        total = jnp.sum(x * x, axis=-1, keepdims=True)
        XS[pl.ds(b * block, block), :] = nt(h, HX[pl.ds(hr, 128), :]) + jnp.where(
            iota((block, 128), 1) == 80, total, 0.0
        )

    pl.semaphore_wait(barrier, nf - 1 + nc)
    swap = pltpu.make_async_remote_copy(
        src_ref=XS, dst_ref=XR, send_sem=sec_s, recv_sem=sec_r,
        device_id=(1 - sec, frm, clip), device_id_type=MESH,
    )
    swap.start()

    load(5)
    when = iota((line, 128), 0)
    own = jnp.broadcast_to(ids[...].astype(F32), (128, line)).T
    mt1 = jnp.where((own == pltpu.roll(own, 1, 0)) & (when >= 1), 1.0, 0.0)
    mt2 = jnp.where((own == pltpu.roll(own, 2, 0)) & (when >= 2), 1.0, 0.0)
    mt1u = pltpu.roll(mt1, line - 1, 0)
    mt2u = pltpu.roll(mt2, line - 2, 0)
    masks = jnp.concatenate([mt1, mt2, mt1u, mt2u], axis=1)
    MT[...] = masks
    REP[...] = one_hot(iota((rows, line), 0) // 4 == iota((rows, line), 1))
    MS[...] = nn(REP[...], masks.astype(BF))

    WD[...] = jnp.zeros(WD.shape, BF)
    WD[pl.ds(0, LO), pl.ds(0, LO)] = w_two[0]
    WD[pl.ds(0, LO), pl.ds(128, LO)] = w_two[1]
    WD[pl.ds(128, LO), pl.ds(128, LO)] = w_two[0]
    WD[pl.ds(256, LO), pl.ds(0, LO)] = w_two[2]
    WD[pl.ds(384, LO), pl.ds(0, LO)] = w_two[1]
    WD[pl.ds(384, LO), pl.ds(128, LO)] = w_two[2]
    WI[...] = jnp.zeros(WI.shape, BF)
    for k in range(3):
        for s in range(4):
            WI[pl.ds(128 * k + 16 * s, 16), :] = w_in[k]
    G2[...] = jnp.zeros(G2.shape, F32)
    G2[:, pl.ds(0, LO)] = jnp.broadcast_to(gain2[...].reshape(1, LO), (8, LO))
    U[pl.ds(0, 8), :] = jnp.zeros((8, 768), F32)
    HS[pl.ds(rows, 8), :] = jnp.zeros((8, 512), F32)
    JL[pl.ds(rows, 8), :] = jnp.zeros((8, 3 * HI), F32)

    for i in range(2):
        SRC[pl.ds(128 * i + LO, 128 - LO), :] = jnp.zeros((128 - LO, rows), BF)
    for k in range(6):
        WUP[pl.ds(128 * k + LO, 128 - LO), :] = jnp.zeros((128 - LO, HI), BF)
    load(2)
    to_row = iota((rows, rows), 0)
    from_row = iota((rows, rows), 1)
    perm = one_hot(from_row == ((to_row & 15) // 4) * edge + (to_row // 16) * 4 + (to_row & 3))
    SR[...] = nt(perm, SRC[...]).astype(BF).reshape(nf, 16, 256)
    load(3)

    swap.wait()
    ST[...] = XS[...] + XR[...]
    consts = ST[pl.ds(hr + 64, 16), :]
    col_sum = consts[0:1, :]
    sw = consts[8:9, :]
    stats = ST[pl.ds(0, hr), :]
    mean = stats[:, 64:65] * (1.0 / dd)
    inv = lax.rsqrt(stats[:, 80:81] * (1.0 / dd) - mean * mean + EPS)
    hl = iota((hr, 128), 1)
    pay = jnp.where(hl < 64, inv * (stats - mean * col_sum), jnp.where(hl == 64, inv, 0.0))
    XS[pl.ds(0, hr), :] = pay
    for j in range(4):
        X2[:, j, :] = XS[pl.ds(pl.multiple_of(j * 2 * nf + sec * nf, 8) if nf % 8 == 0 else j * 2 * nf + sec * nf, nf), :]
    to_all(X2, RX, lat_s, lat_r)
    to_all(SR, RW, rew_s, rew_r)
    RX[pl.ds(frm, 1)] = X2[pl.ds(frm, 1)]
    RW[pl.ds(frm, 1)] = SR[pl.ds(frm, 1)]
    all_of(X2, RX, lat_s, lat_r).wait_recv()

    for j in range(4):
        LTS[pl.ds(j, nf, stride=4), :] = RX[:, j, :]
    tl = iota((line, 128), 1)
    lat = jnp.where(tl < 64, LTS[...] + sw, 0.0)
    lat = lat.astype(BF).astype(F32)
    cat = jnp.concatenate(
        [lat, MT[:, 0:128] * pltpu.roll(lat, 1, 0), MT[:, 128:256] * pltpu.roll(lat, 2, 0)], axis=1
    ).astype(BF)
    mine = ((iota((rows, HI), 1) & 127) // 16) == (iota((rows, HI), 0) & 3)
    spread = jnp.where(mine, nn(REP[...], cat), 0.0).astype(BF)
    B[...] = nn(spread, WI[...])
    g1 = gain1[...].reshape(1, HI)

    def act_one(b, carry):
        at = pl.multiple_of(b * RB, RB)
        act = nb(B[pl.ds(at, RB), :], g1, HI)
        ext = jnp.concatenate([carry, act], axis=0)
        m1 = tile(MS[pl.ds(at, RB), 0:128], 3)
        m2 = tile(MS[pl.ds(at, RB), 128:256], 3)
        AC[pl.ds(at, RB), 0:HI] = act.astype(BF)
        AC[pl.ds(at, RB), HI : 2 * HI] = (ext[4 : RB + 4] * m1).astype(BF)
        AC[pl.ds(at, RB), 2 * HI : 3 * HI] = (ext[0:RB] * m2).astype(BF)
        return ext[RB:]

    lax.fori_loop(0, steps, act_one, jnp.zeros((8, HI), F32), unroll=True)
    load(4)
    TR[...] = (B[...] + nn(AC[...], W1[...])).astype(BF)
    U[pl.ds(8, rows), :] = nt(TR[...], WUP[...])
    g2 = G2[0:1, :]

    def act_two(b, carry):
        at = pl.multiple_of(b * RB, RB)
        m1 = tile(MS[pl.ds(at, RB), 0:128], 2)
        m2 = tile(MS[pl.ds(at, RB), 128:256], 2)
        one = U[pl.ds(at, RB + 8), 256:512]
        two = U[pl.ds(at, RB + 8), 512:768]
        up = U[pl.ds(at + 8, RB), 0:256] + one[4 : RB + 4] * m1 + two[0:RB] * m2
        UP[pl.ds(at, RB), :] = up
        act = jnp.concatenate([nb(up[:, :128], g2, LO), nb(up[:, 128:], g2, LO)], axis=1)
        ext = jnp.concatenate([carry, act], axis=0)
        A2[pl.ds(at, RB), 0:256] = act.astype(BF)
        A2[pl.ds(at, RB), 256:512] = (ext[4 : RB + 4] * m1).astype(BF)
        return ext[RB:]

    lax.fori_loop(0, steps, act_two, jnp.zeros((8, 256), F32), unroll=True)
    DEC[...] = (UP[...] + nn(A2[...], WD[...])).astype(BF).reshape(nf, 16, 256)
    to_all(DEC, RD, dec_s, dec_r, slice(0, 16))
    RD[pl.ds(frm, 1)] = DEC[pl.ds(frm, 1)]

    all_of(SR, RW, rew_s, rew_r).wait_recv()
    HS[pl.ds(0, rows), :] = nt(RW[...].reshape(rows, 256), WD[...])

    def up_grad(b, c):
        at = pl.multiple_of(b * RB, RB)
        m1 = tile(MS[pl.ds(at, RB), 256:384], 2)
        later = HS[pl.ds(at, RB + 8), 256:512]
        second = HS[pl.ds(at, RB), 0:256] + later[4 : RB + 4] * m1
        up = UP[pl.ds(at, RB), :]
        g = RW[pl.ds(b * (RB // 16), RB // 16)].reshape(RB, 256).astype(F32)
        back = [nb_back(second[:, i : i + 128], up[:, i : i + 128], g2, LO) for i in (0, 128)]
        UG[pl.ds(at, RB), :] = (g + jnp.concatenate(back, axis=1)).astype(BF)
        return c

    lax.fori_loop(0, steps, up_grad, 0, unroll=True)
    for k in range(3):
        JL[pl.ds(0, rows), HI * k : HI * k + HI] = nn(UG[...], WUP[pl.ds(256 * k, 256), :])

    def gathered(at):
        m1 = tile(MS[pl.ds(at, RB), 256:384], 3)
        m2 = tile(MS[pl.ds(at, RB), 384:512], 3)
        one = JL[pl.ds(at, RB + 8), HI : 2 * HI]
        two = JL[pl.ds(at, RB + 8), 2 * HI : 3 * HI]
        return JL[pl.ds(at, RB), 0:HI] + one[4 : RB + 4] * m1 + two[8 : RB + 8] * m2

    def trunk_grad(b, c):
        at = pl.multiple_of(b * RB, RB)
        TG[pl.ds(at, RB), :] = gathered(at).astype(BF)
        return c

    lax.fori_loop(0, steps, trunk_grad, 0, unroll=True)
    JL[pl.ds(0, rows), :] = nt(TG[...], W1[...])

    def base_grad(b, c):
        at = pl.multiple_of(b * RB, RB)
        back = nb_back(gathered(at), B[pl.ds(at, RB), :], g1, HI)
        BG[pl.ds(at, RB), :] = (TG[pl.ds(at, RB), :].astype(F32) + back).astype(BF)
        return c

    lax.fori_loop(0, steps, base_grad, 0, unroll=True)
    ZM[...] = jnp.where(mine, nt(BG[...], WI[...]), 0.0).astype(BF)
    rep_t = one_hot(iota((line, rows), 0) == iota((line, rows), 1) // 4)
    y = nn(rep_t, ZM[...])
    lg = y[:, 0:128]
    lg = lg + MT[:, 256:384] * pltpu.roll(y[:, 128:256], line - 1, 0)
    lg = lg + MT[:, 384:512] * pltpu.roll(y[:, 256:384], line - 2, 0)
    lgb = lg.astype(BF)
    lg = lgb.astype(F32)

    pre = LTS[...]
    inv_t = pre[:, 64:65]
    first = jnp.sum(lg * col_sum, axis=-1, keepdims=True) * (1.0 / dd)
    second = jnp.sum(lg * pre, axis=-1, keepdims=True) * (1.0 / dd)
    gram = ST[pl.ds(hr, 64), :]
    gram_hi = gram.astype(BF)
    gram_lo = (gram - gram_hi.astype(F32)).astype(BF)
    quad = nn(lgb[:, 0:64], gram_hi) + nn(lgb[:, 0:64], gram_lo)
    quad = jnp.sum(lg * quad, axis=-1, keepdims=True)
    inv_sq = inv_t * inv_t
    part = inv_sq * (quad - dd * (first * first + second * second * (1.0 + EPS * inv_sq)))
    part = jnp.sum(part, axis=0, keepdims=True)
    PS[...] = jnp.where(
        tl < 64, lg, jnp.where(tl == 64, first, jnp.where(tl == 65, second, jnp.where(tl == 66, part, 0.0)))
    )
    for j in range(4):
        X3[:, j, :] = PS[pl.ds(j, nf, stride=4), :]
    half = RXA.at[sec]
    to_all(X3, half, lg_s, lg_r)
    half[pl.ds(frm, 1)] = X3[pl.ds(frm, 1)]
    all_of(X3, half, lg_s, lg_r).wait_recv()

    trade = pltpu.make_async_remote_copy(
        src_ref=RXA.at[sec], dst_ref=RXA.at[sec], send_sem=sx_s, recv_sem=sx_r,
        device_id=(1 - sec, frm, clip), device_id_type=MESH,
    )
    trade.start()
    to_all(DEC, RD, dec_s, dec_r, slice(16, None))
    trade.wait()
    everyone = jnp.sum(RXA[0, :, 0, :] + RXA[1, :, 0, :], axis=0, keepdims=True)
    ZS[...] = everyone
    for d in above:
        pltpu.make_async_remote_copy(
            src_ref=ZS, dst_ref=ZB.at[clip], send_sem=z_s, recv_sem=z_r,
            device_id=(sec, frm, d), device_id_type=MESH,
        ).start()
    ZB[pl.ds(clip, 1)] = everyone.reshape(1, 1, 128)

    for j in range(4):
        for s in range(2):
            FIN[pl.ds(j * 2 * nf + s * nf, nf), :] = RXA[s, :, j, :]
    got = FIN[...]
    a = got[:, 64:65]
    b = got[:, 65:66]
    stats = ST[pl.ds(0, hr), :]
    mean = stats[:, 64:65] * (1.0 / dd)
    inv = lax.rsqrt(stats[:, 80:81] * (1.0 / dd) - mean * mean + EPS)
    KB[0] = jnp.broadcast_to(inv, (hr, 128))
    KB[1] = jnp.broadcast_to(inv * (inv * b * mean - a), (hr, 128))
    KB[2] = jnp.broadcast_to(inv * inv * b, (hr, 128))
    gotb = got[:, 0:64].astype(BF)

    def token_grad(c, carry):
        at = pl.ds(pl.multiple_of(c * 256, 256), 256)
        grads = nn(gotb, HX[pl.ds(hr, 64), at])
        h = HX[pl.ds(0, hr), at].astype(F32)
        RAW[:, at] = (grads * tile(KB[0], 2) + tile(KB[1], 2) - h * tile(KB[2], 2)).astype(BF)
        return carry

    lax.fori_loop(0, HX.shape[1] // 256, token_grad, 0, unroll=2)
    out_raw = pltpu.make_async_copy(RAW, raw, lsem.at[0])
    out_raw.start()

    all_of(DEC, RD, dec_s, dec_r).wait_recv()
    same = one_hot(iota((256, 256), 0) == iota((256, 256), 1))
    turned = nt(same, RD[...].reshape(rows, 256)).astype(BF)
    perm = one_hot(to_row == ((from_row // edge) * 4) + (lax.rem(from_row, edge) // 4) * 16 + (from_row & 3))
    turned = nn(turned, perm).astype(BF)
    for j in range(4):
        for i in range(2):
            DT[2 * j + i] = turned[128 * i : 128 * i + LO, j * edge : (j + 1) * edge]

    out_dec = pltpu.make_async_copy(DT, dect, lsem.at[1])
    out_dec.start()

    z_all = pltpu.make_async_remote_copy(
        src_ref=ZB.at[pl.ds(0, nc - 1)], dst_ref=ZB.at[pl.ds(0, nc - 1)],
        send_sem=z_s, recv_sem=z_r, device_id=(sec, frm, clip), device_id_type=MESH,
    )
    z_all.wait_recv()
    total = jnp.sum(ZB[:, 0, :], axis=0, keepdims=True)[:, 66:67]
    grow = lax.rsqrt(jnp.maximum(total, 0.0) * (1.0 / count) + EPS)
    SC[...] = jnp.broadcast_to(grow, (8, 128))
    out_scale = pltpu.make_async_copy(SC, scale_out, lsem.at[2])
    out_scale.start()
    out_scale.wait()
    out_raw.wait()
    out_dec.wait()

    all_of(X2, RX, lat_s, lat_r).wait_send()
    all_of(SR, RW, rew_s, rew_r).wait_send()
    all_of(DEC, RD, dec_s, dec_r).wait_send()
    all_of(X3, half, lg_s, lg_r).wait_send()
    z_all.wait_send()


def last_kernel(parts, raw, scale_h, dect, out, decoded, got, done, dec, scale, sems):
    factor = pltpu.make_async_copy(scale_h, scale, sems.at[1 + 2 * parts])
    factor.start()
    size = got.shape[0] // parts
    inward = pltpu.make_async_copy(dect, dec, sems.at[0])
    outward = pltpu.make_async_copy(dec, decoded, sems.at[0])
    spots = [pl.ds(p * size, size) for p in range(parts)]
    reads = [pltpu.make_async_copy(raw.at[at], got.at[at], sems.at[1 + p]) for p, at in enumerate(spots)]
    for read in reads:
        read.start()
    inward.start()
    factor.wait()
    writes = []
    for p, at in enumerate(spots):
        reads[p].wait()
        done[at, :] = (got[at, :].astype(F32) * scale[0:1, 0:1]).astype(BF)
        writes.append(pltpu.make_async_copy(done.at[at], out.at[at], sems.at[1 + parts + p]))
        writes[-1].start()
    inward.wait()
    outward.start()
    for write in writes:
        write.wait()
    outward.wait()


def body(nf, nc, dd, count, hidden, modulation, head_w, clip_ids, w_in, gain_one, w_one, w_up, gain_two, w_two, reward_grad):
    wide = hidden.shape[3]
    rows, line, hr = 16 * nf, 4 * nf, 8 * nf
    hid = hidden.reshape(hr, wide)
    hbm = pl.BlockSpec(memory_space=pltpu.HBM)
    dma = pltpu.SemaphoreType.DMA
    V = pltpu.VMEM
    raw, scale, dect = pl.pallas_call(
        functools.partial(main_kernel, nf, nc, dd, count),
        out_shape=(
            jax.ShapeDtypeStruct((hr, wide), BF),
            jax.ShapeDtypeStruct((8, 128), F32),
            jax.ShapeDtypeStruct((8, LO, 4 * nf), BF),
        ),
        in_specs=[hbm] * 11,
        out_specs=(hbm, hbm, hbm),
        scratch_shapes=[
            V((hr + 128, wide), BF),
            V((64, wide), BF),
            V((3 * HI, HI), BF),
            V((hr + 80, 128), F32),
            V((hr + 80, 128), F32),
            V((nf, 4, 128), F32),
            V((nf, 4, 128), F32),
            V((256, rows), BF),
            V((nf, 16, 256), BF),
            V((nf, 16, 256), BF),
            V((line, 128), F32),
            V((line, 512), F32),
            V((rows, 512), F32),
            V((rows, line), BF),
            V((512, 256), BF),
            V((HI, HI), BF),
            V((768, HI), BF),
            V((8, 128), F32),
            V((rows, HI), F32),
            V((rows, 3 * HI), BF),
            V((rows, HI), BF),
            V((rows + 8, 768), F32),
            V((rows, 256), F32),
            V((rows, 512), BF),
            V((nf, 16, 256), BF),
            V((rows + 8, 512), F32),
            V((rows, 256), BF),
            V((rows + 8, 3 * HI), F32),
            V((rows, HI), BF),
            V((rows, HI), BF),
            V((rows, HI), BF),
            V((line, 128), F32),
            V((nf, 4, 128), F32),
            V((2, nf, 4, 128), F32),
            V((1, 128), F32),
            V((nc, 1, 128), F32),
            V((hr + 80, 128), F32),
            V((nf, 16, 256), BF),
            V((hr, 128), F32),
            V((3, hr, 128), F32),
            V((hr, wide), BF),
            V((8, LO, 4 * nf), BF),
            V((2, wide), F32),
            V((1, line), jnp.int32),
            V((3, 16, HI), BF),
            V((HI,), F32),
            V((LO,), F32),
            V((3, LO, LO), BF),
            V((8, 128), F32),
            dma((26,)),
        ]
        + [dma] * 14,
        compiler_params=pltpu.CompilerParams(
            collective_id=0, has_side_effects=True, vmem_limit_bytes=60 * 1024 * 1024
        ),
        name="exchange",
    )(
        hid, modulation[0], head_w.T, clip_ids, w_in, gain_one, w_one.reshape(3 * HI, HI),
        jnp.transpose(w_up, (0, 2, 1)), gain_two, w_two, jnp.transpose(reward_grad[0], (0, 2, 1)),
    )
    parts = min(4, hr // 16)
    grad, dect = pl.pallas_call(
        functools.partial(last_kernel, parts),
        out_shape=(
            jax.ShapeDtypeStruct((hr, wide), BF),
            jax.ShapeDtypeStruct((8, LO, 4 * nf), BF),
        ),
        in_specs=[hbm, hbm, hbm],
        out_specs=(hbm, hbm),
        scratch_shapes=[V((hr, wide), BF), V((hr, wide), BF), V((8, LO, 4 * nf), BF), V((8, 128), F32), dma((2 + 2 * parts,))],
        compiler_params=pltpu.CompilerParams(vmem_limit_bytes=60 * 1024 * 1024),
        name="finish",
    )(raw, scale, dect)
    return jnp.transpose(dect, (0, 2, 1))[None], grad.reshape(hidden.shape)


def solution(mesh):
    nf, nc = mesh.shape["frm"], mesh.shape["clip"]

    def whole(hidden, *rest):
        dd = hidden.shape[3]
        count = float(hidden.size)
        in_specs = (
            P("clip", "frm", None, "sec"),
            P("clip", None, "sec"),
            P("sec", None),
            P("clip", None),
            P(),
            P(),
            P(),
            P(),
            P(),
            P(),
            P("clip", "frm", "sec", None),
        )
        out_specs = (P("clip", "frm", "sec", None), P("clip", "frm", None, "sec"))
        return jax.shard_map(
            functools.partial(body, nf, nc, dd, count),
            mesh=mesh, in_specs=in_specs, out_specs=out_specs, check_vma=False,
        )(hidden, *rest)

    return whole
```

```python
import functools

import jax
import jax.numpy as jnp
from jax import lax
from jax.experimental import pallas as pl
from jax.experimental.pallas import tpu as pltpu
from jax.sharding import PartitionSpec as P

BF = jnp.bfloat16
F32 = jnp.float32
MESH = pl.DeviceIdType.MESH
HI = 384
LO = 96
EPS = 1e-6
RB = 64


def nn(a, b):
    return jnp.dot(a, b, preferred_element_type=F32)


def nt(a, b):
    return lax.dot_general(a, b, (((1,), (1,)), ((), ())), preferred_element_type=F32)


def iota(shape, dim):
    return lax.broadcasted_iota(jnp.int32, shape, dim)


def one_hot(cond):
    return jnp.where(cond, 1.0, 0.0).astype(BF)


def sigmoid(x):
    return 0.5 * jnp.tanh(0.5 * x) + 0.5


def tile(mask, times):
    return jnp.concatenate([mask] * times, axis=1)


def nb(x, gain, width):
    r = lax.rsqrt(jnp.sum(x * x, axis=-1, keepdims=True) * (1.0 / width) + EPS)
    n = x * r * gain
    return n * sigmoid(n)


def nb_back(g, x, gain, width):
    r = lax.rsqrt(jnp.sum(x * x, axis=-1, keepdims=True) * (1.0 / width) + EPS)
    n = x * r * gain
    sg = sigmoid(n)
    u = g * sg * (1.0 + n * (1.0 - sg)) * gain
    mixed = jnp.sum(u * x, axis=-1, keepdims=True) * (1.0 / width)
    return r * u - x * (r * r * r * mixed)


def main_kernel(
    nf, nc, dd, count,
    hidden, mod_h, head_w, ids_h, w_in_h, gain1_h, w_one, w_up, gain2_h, w_two_h, reward,
    raw, scale_out, dect,
    HX, HW, W1, XS, XR, X2, RX, SRC, SR, RW, LTS, MT, MS, REP, WD, WI, WUP, G2,
    B, AC, TR, U, UP, A2, DEC, HS, UG, JL, TG, BG, ZM, PS, X3, RXA, ZS, ZB, ST, RD, FIN, KB, RAW, DT, mod, ids, w_in, gain1, gain2, w_two, SC,
    lsem, sec_s, sec_r, lat_s, lat_r, rew_s, rew_r, dec_s, dec_r, lg_s, lg_r, sx_s, sx_r, z_s, z_r,
):
    sec = lax.axis_index("sec")
    frm = lax.axis_index("frm")
    clip = lax.axis_index("clip")
    rows = 16 * nf
    line = 4 * nf
    hr = 8 * nf
    steps = rows // RB

    edge = 4 * nf
    loads = [
        [pltpu.make_async_copy(head_w, HW, lsem.at[0]), pltpu.make_async_copy(mod_h, mod, lsem.at[20])],
        [pltpu.make_async_copy(hidden, HX.at[pl.ds(0, hr)], lsem.at[1])],
        [
            pltpu.make_async_copy(
                reward.at[2 * j + i], SRC.at[pl.ds(128 * i, LO), pl.ds(j * edge, edge)], lsem.at[6 + 2 * j + i]
            )
            for j in range(4) for i in range(2)
        ],
        [
            pltpu.make_async_copy(
                w_up.at[k, pl.ds(LO * i, LO)], WUP.at[pl.ds(256 * k + 128 * i, LO)], lsem.at[14 + 2 * k + i]
            )
            for k in range(3) for i in range(2)
        ],
        [pltpu.make_async_copy(w_one, W1, lsem.at[4])],
        [
            pltpu.make_async_copy(src, dst, lsem.at[21 + i])
            for i, (src, dst) in enumerate(
                ((ids_h, ids), (w_in_h, w_in), (gain1_h, gain1), (gain2_h, gain2), (w_two_h, w_two))
            )
        ],
    ]

    def load(which):
        for copy in loads[which]:
            copy.wait()

    for group in loads[:2]:
        for copy in group:
            copy.start()

    nx = 4
    ny = nf // nx
    yy, xx = frm // nx, lax.rem(frm, nx)
    ways = [(min(dy, ny - dy) + min(dx, nx - dx), dy, dx) for dy in range(ny) for dx in range(nx) if dy or dx]
    seen = {}
    far = []
    for hop, dy, dx in sorted(ways, reverse=True):
        side = (hop, 2 * dy > ny)
        seen[side] = seen.get(side, 0) + 1
        far.append((-hop, seen[side], dy, dx))
    far = [(-hop, dy, dx) for hop, _, dy, dx in sorted(far)]
    peers = [lax.rem(yy + dy, ny) * nx + lax.rem(xx + dx, nx) for _, dy, dx in far]
    above = [lax.rem(clip + dz, nc) for dz in sorted(range(1, nc), key=lambda dz: -min(dz, nc - dz))]

    barrier = pltpu.get_barrier_semaphore()
    for d in peers:
        pl.semaphore_signal(barrier, inc=1, device_id=(sec, d, clip), device_id_type=MESH)
    for d in above:
        pl.semaphore_signal(barrier, inc=1, device_id=(sec, frm, d), device_id_type=MESH)
    pl.semaphore_signal(barrier, inc=1, device_id=(1 - sec, frm, clip), device_id_type=MESH)
    for group in loads[2:]:
        for copy in group:
            copy.start()

    def to_all(src, dst, ssem, rsem, some=slice(None)):
        for d in peers[some]:
            pltpu.make_async_remote_copy(
                src_ref=src.at[d], dst_ref=dst.at[frm], send_sem=ssem, recv_sem=rsem,
                device_id=(sec, d, clip), device_id_type=MESH,
            ).start()

    def all_of(src, dst, ssem, rsem):
        return pltpu.make_async_remote_copy(
            src_ref=src.at[pl.ds(0, nf - 1)], dst_ref=dst.at[pl.ds(0, nf - 1)],
            send_sem=ssem, recv_sem=rsem, device_id=(sec, frm, clip), device_id_type=MESH,
        )

    HX[pl.ds(hr + 64, 16), :] = jnp.ones((16, HX.shape[1]), BF)
    HX[pl.ds(hr + 80, 48), :] = jnp.zeros((48, HX.shape[1]), BF)
    load(0)
    shift = mod[0:1, :]
    HX[pl.ds(hr, 64), :] = (HW[...].astype(F32) * (1.0 + mod[1:2, :])).astype(BF)
    coarse = shift.astype(BF).astype(F32)
    pick = iota((16, HX.shape[1]), 0)
    pair = jnp.where(pick == 0, coarse, jnp.where(pick == 1, shift - coarse, 0.0)).astype(BF)
    shifted = nt(pair, HW[...])
    XS[pl.ds(hr, 80), :] = nt(HX[pl.ds(hr, 80), :], HX[pl.ds(hr, 128), :])
    XS[pl.ds(hr + 72, 8), pl.ds(0, 64)] = jnp.broadcast_to(shifted[0:1, :] + shifted[1:2, :], (8, 64))

    load(1)
    block = min(hr, 64)
    for b in range(hr // block):
        h = HX[pl.ds(b * block, block), :]
        x = h.astype(F32)
        total = jnp.sum(x * x, axis=-1, keepdims=True)
        XS[pl.ds(b * block, block), :] = nt(h, HX[pl.ds(hr, 128), :]) + jnp.where(
            iota((block, 128), 1) == 80, total, 0.0
        )

    pl.semaphore_wait(barrier, nf - 1 + nc)
    swap = pltpu.make_async_remote_copy(
        src_ref=XS, dst_ref=XR, send_sem=sec_s, recv_sem=sec_r,
        device_id=(1 - sec, frm, clip), device_id_type=MESH,
    )
    swap.start()

    load(5)
    when = iota((line, 128), 0)
    own = jnp.broadcast_to(ids[...].astype(F32), (128, line)).T
    mt1 = jnp.where((own == pltpu.roll(own, 1, 0)) & (when >= 1), 1.0, 0.0)
    mt2 = jnp.where((own == pltpu.roll(own, 2, 0)) & (when >= 2), 1.0, 0.0)
    mt1u = pltpu.roll(mt1, line - 1, 0)
    mt2u = pltpu.roll(mt2, line - 2, 0)
    masks = jnp.concatenate([mt1, mt2, mt1u, mt2u], axis=1)
    MT[...] = masks
    REP[...] = one_hot(iota((rows, line), 0) // 4 == iota((rows, line), 1))
    MS[...] = nn(REP[...], masks.astype(BF))

    WD[...] = jnp.zeros(WD.shape, BF)
    WD[pl.ds(0, LO), pl.ds(0, LO)] = w_two[0]
    WD[pl.ds(0, LO), pl.ds(128, LO)] = w_two[1]
    WD[pl.ds(128, LO), pl.ds(128, LO)] = w_two[0]
    WD[pl.ds(256, LO), pl.ds(0, LO)] = w_two[2]
    WD[pl.ds(384, LO), pl.ds(0, LO)] = w_two[1]
    WD[pl.ds(384, LO), pl.ds(128, LO)] = w_two[2]
    WI[...] = jnp.zeros(WI.shape, BF)
    for k in range(3):
        for s in range(4):
            WI[pl.ds(128 * k + 16 * s, 16), :] = w_in[k]
    G2[...] = jnp.zeros(G2.shape, F32)
    G2[:, pl.ds(0, LO)] = jnp.broadcast_to(gain2[...].reshape(1, LO), (8, LO))
    U[pl.ds(0, 8), :] = jnp.zeros((8, 768), F32)
    HS[pl.ds(rows, 8), :] = jnp.zeros((8, 512), F32)
    JL[pl.ds(rows, 8), :] = jnp.zeros((8, 3 * HI), F32)

    for i in range(2):
        SRC[pl.ds(128 * i + LO, 128 - LO), :] = jnp.zeros((128 - LO, rows), BF)
    for k in range(6):
        WUP[pl.ds(128 * k + LO, 128 - LO), :] = jnp.zeros((128 - LO, HI), BF)
    load(2)
    to_row = iota((rows, rows), 0)
    from_row = iota((rows, rows), 1)
    perm = one_hot(from_row == ((to_row & 15) // 4) * edge + (to_row // 16) * 4 + (to_row & 3))
    SR[...] = nt(perm, SRC[...]).astype(BF).reshape(nf, 16, 256)
    load(3)

    swap.wait()
    ST[pl.ds(hr, 80), :] = XS[pl.ds(hr, 80), :] + XR[pl.ds(hr, 80), :]
    consts = ST[pl.ds(hr + 64, 16), :]
    col_sum = consts[0:1, :]
    sw = consts[8:9, :]
    own_half = sec * nf
    hl = iota((hr, 128), 1)
    nl = iota((nf, 128), 1)
    for j in range(4):
        at = pl.ds(pl.multiple_of(j * 2 * nf + own_half, 8) if nf % 8 == 0 else j * 2 * nf + own_half, nf)
        stats = XS[at, :] + XR[at, :]
        mean = stats[:, 64:65] * (1.0 / dd)
        inv = lax.rsqrt(stats[:, 80:81] * (1.0 / dd) - mean * mean + EPS)
        X2[:, j, :] = jnp.where(nl < 64, inv * (stats - mean * col_sum), jnp.where(nl == 64, inv, 0.0))
    to_all(X2, RX, lat_s, lat_r)
    to_all(SR, RW, rew_s, rew_r)
    ST[pl.ds(0, hr), :] = XS[pl.ds(0, hr), :] + XR[pl.ds(0, hr), :]
    RX[pl.ds(frm, 1)] = X2[pl.ds(frm, 1)]
    RW[pl.ds(frm, 1)] = SR[pl.ds(frm, 1)]
    all_of(X2, RX, lat_s, lat_r).wait_recv()

    for j in range(4):
        LTS[pl.ds(j, nf, stride=4), :] = RX[:, j, :]
    tl = iota((line, 128), 1)
    lat = jnp.where(tl < 64, LTS[...] + sw, 0.0)
    lat = lat.astype(BF).astype(F32)
    cat = jnp.concatenate(
        [lat, MT[:, 0:128] * pltpu.roll(lat, 1, 0), MT[:, 128:256] * pltpu.roll(lat, 2, 0)], axis=1
    ).astype(BF)
    mine = ((iota((rows, HI), 1) & 127) // 16) == (iota((rows, HI), 0) & 3)
    spread = jnp.where(mine, nn(REP[...], cat), 0.0).astype(BF)
    B[...] = nn(spread, WI[...])
    g1 = gain1[...].reshape(1, HI)

    def act_one(b, carry):
        at = pl.multiple_of(b * RB, RB)
        act = nb(B[pl.ds(at, RB), :], g1, HI)
        ext = jnp.concatenate([carry, act], axis=0)
        m1 = tile(MS[pl.ds(at, RB), 0:128], 3)
        m2 = tile(MS[pl.ds(at, RB), 128:256], 3)
        AC[pl.ds(at, RB), 0:HI] = act.astype(BF)
        AC[pl.ds(at, RB), HI : 2 * HI] = (ext[4 : RB + 4] * m1).astype(BF)
        AC[pl.ds(at, RB), 2 * HI : 3 * HI] = (ext[0:RB] * m2).astype(BF)
        return ext[RB:]

    lax.fori_loop(0, steps, act_one, jnp.zeros((8, HI), F32), unroll=True)
    load(4)
    TR[...] = (B[...] + nn(AC[...], W1[...])).astype(BF)
    U[pl.ds(8, rows), :] = nt(TR[...], WUP[...])
    g2 = G2[0:1, :]

    def act_two(b, carry):
        at = pl.multiple_of(b * RB, RB)
        m1 = tile(MS[pl.ds(at, RB), 0:128], 2)
        m2 = tile(MS[pl.ds(at, RB), 128:256], 2)
        one = U[pl.ds(at, RB + 8), 256:512]
        two = U[pl.ds(at, RB + 8), 512:768]
        up = U[pl.ds(at + 8, RB), 0:256] + one[4 : RB + 4] * m1 + two[0:RB] * m2
        UP[pl.ds(at, RB), :] = up
        act = jnp.concatenate([nb(up[:, :128], g2, LO), nb(up[:, 128:], g2, LO)], axis=1)
        ext = jnp.concatenate([carry, act], axis=0)
        A2[pl.ds(at, RB), 0:256] = act.astype(BF)
        A2[pl.ds(at, RB), 256:512] = (ext[4 : RB + 4] * m1).astype(BF)
        return ext[RB:]

    lax.fori_loop(0, steps, act_two, jnp.zeros((8, 256), F32), unroll=True)
    DEC[...] = (UP[...] + nn(A2[...], WD[...])).astype(BF).reshape(nf, 16, 256)
    to_all(DEC, RD, dec_s, dec_r, slice(0, 20))
    RD[pl.ds(frm, 1)] = DEC[pl.ds(frm, 1)]

    all_of(SR, RW, rew_s, rew_r).wait_recv()
    HS[pl.ds(0, rows), :] = nt(RW[...].reshape(rows, 256), WD[...])

    def up_grad(b, c):
        at = pl.multiple_of(b * RB, RB)
        m1 = tile(MS[pl.ds(at, RB), 256:384], 2)
        later = HS[pl.ds(at, RB + 8), 256:512]
        second = HS[pl.ds(at, RB), 0:256] + later[4 : RB + 4] * m1
        up = UP[pl.ds(at, RB), :]
        g = RW[pl.ds(b * (RB // 16), RB // 16)].reshape(RB, 256).astype(F32)
        back = [nb_back(second[:, i : i + 128], up[:, i : i + 128], g2, LO) for i in (0, 128)]
        UG[pl.ds(at, RB), :] = (g + jnp.concatenate(back, axis=1)).astype(BF)
        return c

    lax.fori_loop(0, steps, up_grad, 0, unroll=True)
    for k in range(3):
        JL[pl.ds(0, rows), HI * k : HI * k + HI] = nn(UG[...], WUP[pl.ds(256 * k, 256), :])

    def gathered(at):
        m1 = tile(MS[pl.ds(at, RB), 256:384], 3)
        m2 = tile(MS[pl.ds(at, RB), 384:512], 3)
        one = JL[pl.ds(at, RB + 8), HI : 2 * HI]
        two = JL[pl.ds(at, RB + 8), 2 * HI : 3 * HI]
        return JL[pl.ds(at, RB), 0:HI] + one[4 : RB + 4] * m1 + two[8 : RB + 8] * m2

    def trunk_grad(b, c):
        at = pl.multiple_of(b * RB, RB)
        TG[pl.ds(at, RB), :] = gathered(at).astype(BF)
        return c

    lax.fori_loop(0, steps, trunk_grad, 0, unroll=True)
    JL[pl.ds(0, rows), :] = nt(TG[...], W1[...])

    def base_grad(b, c):
        at = pl.multiple_of(b * RB, RB)
        back = nb_back(gathered(at), B[pl.ds(at, RB), :], g1, HI)
        BG[pl.ds(at, RB), :] = (TG[pl.ds(at, RB), :].astype(F32) + back).astype(BF)
        return c

    lax.fori_loop(0, steps, base_grad, 0, unroll=True)
    ZM[...] = jnp.where(mine, nt(BG[...], WI[...]), 0.0).astype(BF)
    rep_t = one_hot(iota((line, rows), 0) == iota((line, rows), 1) // 4)
    y = nn(rep_t, ZM[...])
    lg = y[:, 0:128]
    lg = lg + MT[:, 256:384] * pltpu.roll(y[:, 128:256], line - 1, 0)
    lg = lg + MT[:, 384:512] * pltpu.roll(y[:, 256:384], line - 2, 0)
    lgb = lg.astype(BF)
    lg = lgb.astype(F32)

    pre = LTS[...]
    inv_t = pre[:, 64:65]
    first = jnp.sum(lg * col_sum, axis=-1, keepdims=True) * (1.0 / dd)
    second = jnp.sum(lg * pre, axis=-1, keepdims=True) * (1.0 / dd)
    gram = ST[pl.ds(hr, 64), :]
    gram_hi = gram.astype(BF)
    gram_lo = (gram - gram_hi.astype(F32)).astype(BF)
    quad = nn(lgb[:, 0:64], gram_hi) + nn(lgb[:, 0:64], gram_lo)
    quad = jnp.sum(lg * quad, axis=-1, keepdims=True)
    inv_sq = inv_t * inv_t
    part = inv_sq * (quad - dd * (first * first + second * second * (1.0 + EPS * inv_sq)))
    part = jnp.sum(part, axis=0, keepdims=True)
    PS[...] = jnp.where(
        tl < 64, lg, jnp.where(tl == 64, first, jnp.where(tl == 65, second, jnp.where(tl == 66, part, 0.0)))
    )
    for j in range(4):
        X3[:, j, :] = PS[pl.ds(j, nf, stride=4), :]
    half = RXA.at[sec]
    to_all(X3, half, lg_s, lg_r)
    half[pl.ds(frm, 1)] = X3[pl.ds(frm, 1)]
    all_of(X3, half, lg_s, lg_r).wait_recv()

    trade = pltpu.make_async_remote_copy(
        src_ref=RXA.at[sec], dst_ref=RXA.at[sec], send_sem=sx_s, recv_sem=sx_r,
        device_id=(1 - sec, frm, clip), device_id_type=MESH,
    )
    trade.start()
    to_all(DEC, RD, dec_s, dec_r, slice(20, None))
    trade.wait()
    everyone = jnp.sum(RXA[0, :, 0, :] + RXA[1, :, 0, :], axis=0, keepdims=True)
    ZS[...] = everyone
    for d in above:
        pltpu.make_async_remote_copy(
            src_ref=ZS, dst_ref=ZB.at[clip], send_sem=z_s, recv_sem=z_r,
            device_id=(sec, frm, d), device_id_type=MESH,
        ).start()
    ZB[pl.ds(clip, 1)] = everyone.reshape(1, 1, 128)

    for j in range(4):
        for s in range(2):
            FIN[pl.ds(j * 2 * nf + s * nf, nf), :] = RXA[s, :, j, :]
    got = FIN[...]
    a = got[:, 64:65]
    b = got[:, 65:66]
    stats = ST[pl.ds(0, hr), :]
    mean = stats[:, 64:65] * (1.0 / dd)
    inv = lax.rsqrt(stats[:, 80:81] * (1.0 / dd) - mean * mean + EPS)
    KB[0] = jnp.broadcast_to(inv, (hr, 128))
    KB[1] = jnp.broadcast_to(inv * (inv * b * mean - a), (hr, 128))
    KB[2] = jnp.broadcast_to(inv * inv * b, (hr, 128))
    gotb = got[:, 0:64].astype(BF)

    def token_grad(c, carry):
        at = pl.ds(pl.multiple_of(c * 256, 256), 256)
        grads = nn(gotb, HX[pl.ds(hr, 64), at])
        h = HX[pl.ds(0, hr), at].astype(F32)
        RAW[:, at] = (grads * tile(KB[0], 2) + tile(KB[1], 2) - h * tile(KB[2], 2)).astype(BF)
        return carry

    lax.fori_loop(0, HX.shape[1] // 256, token_grad, 0, unroll=2)
    out_raw = pltpu.make_async_copy(RAW, raw, lsem.at[0])
    out_raw.start()

    all_of(DEC, RD, dec_s, dec_r).wait_recv()
    same = one_hot(iota((256, 256), 0) == iota((256, 256), 1))
    turned = nt(same, RD[...].reshape(rows, 256)).astype(BF)
    perm = one_hot(to_row == ((from_row // edge) * 4) + (lax.rem(from_row, edge) // 4) * 16 + (from_row & 3))
    turned = nn(turned, perm).astype(BF)
    for j in range(4):
        for i in range(2):
            DT[2 * j + i] = turned[128 * i : 128 * i + LO, j * edge : (j + 1) * edge]

    out_dec = pltpu.make_async_copy(DT, dect, lsem.at[1])
    out_dec.start()

    z_all = pltpu.make_async_remote_copy(
        src_ref=ZB.at[pl.ds(0, nc - 1)], dst_ref=ZB.at[pl.ds(0, nc - 1)],
        send_sem=z_s, recv_sem=z_r, device_id=(sec, frm, clip), device_id_type=MESH,
    )
    z_all.wait_recv()
    total = jnp.sum(ZB[:, 0, :], axis=0, keepdims=True)[:, 66:67]
    grow = lax.rsqrt(jnp.maximum(total, 0.0) * (1.0 / count) + EPS)
    SC[...] = jnp.broadcast_to(grow, (8, 128))
    out_scale = pltpu.make_async_copy(SC, scale_out, lsem.at[2])
    out_scale.start()
    out_scale.wait()
    out_raw.wait()
    out_dec.wait()

    all_of(X2, RX, lat_s, lat_r).wait_send()
    all_of(SR, RW, rew_s, rew_r).wait_send()
    all_of(DEC, RD, dec_s, dec_r).wait_send()
    all_of(X3, half, lg_s, lg_r).wait_send()
    z_all.wait_send()


def last_kernel(parts, raw, scale_h, dect, out, decoded, got, done, dec, scale, sems):
    factor = pltpu.make_async_copy(scale_h, scale, sems.at[1 + 2 * parts])
    factor.start()
    size = got.shape[0] // parts
    inward = pltpu.make_async_copy(dect, dec, sems.at[0])
    outward = pltpu.make_async_copy(dec, decoded, sems.at[0])
    spots = [pl.ds(p * size, size) for p in range(parts)]
    reads = [pltpu.make_async_copy(raw.at[at], got.at[at], sems.at[1 + p]) for p, at in enumerate(spots)]
    for read in reads:
        read.start()
    inward.start()
    factor.wait()
    writes = []
    for p, at in enumerate(spots):
        reads[p].wait()
        done[at, :] = (got[at, :].astype(F32) * scale[0:1, 0:1]).astype(BF)
        writes.append(pltpu.make_async_copy(done.at[at], out.at[at], sems.at[1 + parts + p]))
        writes[-1].start()
    inward.wait()
    outward.start()
    for write in writes:
        write.wait()
    outward.wait()


def body(nf, nc, dd, count, hidden, modulation, head_w, clip_ids, w_in, gain_one, w_one, w_up, gain_two, w_two, reward_grad):
    wide = hidden.shape[3]
    rows, line, hr = 16 * nf, 4 * nf, 8 * nf
    hid = hidden.reshape(hr, wide)
    hbm = pl.BlockSpec(memory_space=pltpu.HBM)
    dma = pltpu.SemaphoreType.DMA
    V = pltpu.VMEM
    raw, scale, dect = pl.pallas_call(
        functools.partial(main_kernel, nf, nc, dd, count),
        out_shape=(
            jax.ShapeDtypeStruct((hr, wide), BF),
            jax.ShapeDtypeStruct((8, 128), F32),
            jax.ShapeDtypeStruct((8, LO, 4 * nf), BF),
        ),
        in_specs=[hbm] * 11,
        out_specs=(hbm, hbm, hbm),
        scratch_shapes=[
            V((hr + 128, wide), BF),
            V((64, wide), BF),
            V((3 * HI, HI), BF),
            V((hr + 80, 128), F32),
            V((hr + 80, 128), F32),
            V((nf, 4, 128), F32),
            V((nf, 4, 128), F32),
            V((256, rows), BF),
            V((nf, 16, 256), BF),
            V((nf, 16, 256), BF),
            V((line, 128), F32),
            V((line, 512), F32),
            V((rows, 512), F32),
            V((rows, line), BF),
            V((512, 256), BF),
            V((HI, HI), BF),
            V((768, HI), BF),
            V((8, 128), F32),
            V((rows, HI), F32),
            V((rows, 3 * HI), BF),
            V((rows, HI), BF),
            V((rows + 8, 768), F32),
            V((rows, 256), F32),
            V((rows, 512), BF),
            V((nf, 16, 256), BF),
            V((rows + 8, 512), F32),
            V((rows, 256), BF),
            V((rows + 8, 3 * HI), F32),
            V((rows, HI), BF),
            V((rows, HI), BF),
            V((rows, HI), BF),
            V((line, 128), F32),
            V((nf, 4, 128), F32),
            V((2, nf, 4, 128), F32),
            V((1, 128), F32),
            V((nc, 1, 128), F32),
            V((hr + 80, 128), F32),
            V((nf, 16, 256), BF),
            V((hr, 128), F32),
            V((3, hr, 128), F32),
            V((hr, wide), BF),
            V((8, LO, 4 * nf), BF),
            V((2, wide), F32),
            V((1, line), jnp.int32),
            V((3, 16, HI), BF),
            V((HI,), F32),
            V((LO,), F32),
            V((3, LO, LO), BF),
            V((8, 128), F32),
            dma((26,)),
        ]
        + [dma] * 14,
        compiler_params=pltpu.CompilerParams(
            collective_id=0, has_side_effects=True, vmem_limit_bytes=60 * 1024 * 1024
        ),
        name="exchange",
    )(
        hid, modulation[0], head_w.T, clip_ids, w_in, gain_one, w_one.reshape(3 * HI, HI),
        jnp.transpose(w_up, (0, 2, 1)), gain_two, w_two, jnp.transpose(reward_grad[0], (0, 2, 1)),
    )
    parts = min(4, hr // 16)
    grad, dect = pl.pallas_call(
        functools.partial(last_kernel, parts),
        out_shape=(
            jax.ShapeDtypeStruct((hr, wide), BF),
            jax.ShapeDtypeStruct((8, LO, 4 * nf), BF),
        ),
        in_specs=[hbm, hbm, hbm],
        out_specs=(hbm, hbm),
        scratch_shapes=[V((hr, wide), BF), V((hr, wide), BF), V((8, LO, 4 * nf), BF), V((8, 128), F32), dma((2 + 2 * parts,))],
        compiler_params=pltpu.CompilerParams(vmem_limit_bytes=60 * 1024 * 1024),
        name="finish",
    )(raw, scale, dect)
    return jnp.transpose(dect, (0, 2, 1))[None], grad.reshape(hidden.shape)


def solution(mesh):
    nf, nc = mesh.shape["frm"], mesh.shape["clip"]

    def whole(hidden, *rest):
        dd = hidden.shape[3]
        count = float(hidden.size)
        in_specs = (
            P("clip", "frm", None, "sec"),
            P("clip", None, "sec"),
            P("sec", None),
            P("clip", None),
            P(),
            P(),
            P(),
            P(),
            P(),
            P(),
            P("clip", "frm", "sec", None),
        )
        out_specs = (P("clip", "frm", "sec", None), P("clip", "frm", None, "sec"))
        return jax.shard_map(
            functools.partial(body, nf, nc, dd, count),
            mesh=mesh, in_specs=in_specs, out_specs=out_specs, check_vma=False,
        )(hidden, *rest)

    return whole
```
